256 devices in a mesh: row: 16 (over x, y_lo, core), col: 16 (over y_hi, z).
Axes of the slice: x: 4, y: 4 (y_hi: 2, y_lo: 2; y = y_hi * 2 + y_lo), z: 8, core: 2. Of those that a mesh axis runs over, the one named last changes fastest.
Arguments:
- valence: bfloat16 [256, 96, 96, 96], P(('row', 'col')), may hold values from -6 to 6
- conduction: bfloat16 [256, 96, 96, 96], P(('row', 'col')), may hold values from -6 to 6
- val_energy: float32 [256], replicated, may hold values from -12 to -1
- cond_energy: float32 [256], P(('row', 'col')), may hold values from 0.5 to 20
- sphere_index: int32 [16384], replicated, may hold values from 0 to 884735, as said below
Outputs:
- response: float32 [16384, 16384], P('row', 'col')
The draws below stay inside these ranges and needn't reach their ends.
Inputs may be any that keep to these rules, and one draw needn't show every extreme that they name: `sphere_index`: the entries are distinct. Each names a plane wave whose three integer components lie within -15 to 15; the six plane waves with one component equal to 15 or -15 and the others zero are always among them.
All inputs are finite; a program needn't handle non-finite values.
Results may differ from the reference program's by a relative error of at most 0.004.
Values may be sent and summed in bfloat16 or wider, within the bound.
A program may use at most 128 MiB of HBM per device.

```python
import math
import jax
import jax.numpy as jnp
from jax import lax

NG = 96
NPW = 16384
GMAX = 15
NV_DEV = 1
NC_DEV = 1
STEPS = 2
NV = 256
NC = 256
TOTAL_PAIRS = 512


def draw_sphere_index(key, part):
    key = jax.random.fold_in(key, 11)
    extent = 2 * GMAX + 1
    cells = extent ** 3
    cell_ids = jnp.arange(cells, dtype=jnp.int32)
    x_freq = cell_ids // (extent * extent) - GMAX
    y_freq = cell_ids // extent % extent - GMAX
    z_freq = cell_ids % extent - GMAX
    radius_sq = x_freq * x_freq + y_freq * y_freq + z_freq * z_freq
    tie_break = jax.random.permutation(key, cells).astype(jnp.int32)
    on_axis = (jnp.abs(x_freq) + jnp.abs(y_freq) + jnp.abs(z_freq) == GMAX) & ((jnp.abs(x_freq) == GMAX) | (jnp.abs(y_freq) == GMAX) | (jnp.abs(z_freq) == GMAX))
    scores = jnp.where(on_axis, tie_break - cells, radius_sq * cells + tie_break)
    unused, chosen = lax.top_k(-scores, NPW)
    chosen = chosen.astype(jnp.int32)
    grid_x = x_freq[chosen] % NG
    grid_y = y_freq[chosen] % NG
    grid_z = z_freq[chosen] % NG
    return ((grid_x * NG + grid_y) * NG + grid_z).astype(jnp.int32)


def block_levels(key, shape, shards, least, top_value):
    gain, own = 1.0, jax.random.fold_in(key, 6)
    for dim, shards_of in shards:
        draws = jnp.exp(jax.random.uniform(jax.random.fold_in(own, dim), (shards_of,), jnp.float32, least / len(shards), top_value / len(shards)))
        gain = gain * jnp.repeat(draws, shape[dim] // shards_of).reshape([-1 if axis == dim else 1 for axis in range(len(shape))])
    return gain


def scatter_about(rng, shape, spread, bound, split=(), held_as=jnp.bfloat16):
    entries = jax.random.normal(rng, shape, jnp.float32) * spread
    if len(split) > 0:
        entries = block_levels(rng, shape, split, -0.22, 0.18) * entries
    return jnp.clip(entries, min=-bound, max=bound).astype(held_as)


def setup_inputs(seed: int = 0) -> dict:
    arg_keys = jax.random.split(jax.random.key(seed), 6)
    return {
        "valence": scatter_about(arg_keys[0], (NV, NG, NG, NG), 1.0, 6.0, ((0, 256),)),
        "conduction": scatter_about(arg_keys[1], (NC, NG, NG, NG), 1.0, 6.0, ((0, 256),)),
        "val_energy": jnp.clip(jax.random.uniform(arg_keys[2], (NV,), jnp.float32, -12.0, -1.0), -12.0, -1.0),
        "cond_energy": jnp.clip(0.5 + 19.5 * jax.random.uniform(arg_keys[3], (NC,), jnp.float32) ** block_levels(arg_keys[3], (NC,), ((0, 256),), -0.2, 0.2), 0.5, 20.0),
        "sphere_index": draw_sphere_index(jax.random.fold_in(arg_keys[5], 71), 0),
    }


def pair_rows(valence, conduction, val_energy, cond_energy, sphere_index, block_pair):
    blocks = NV // NV_DEV
    cond_block = block_pair // STEPS
    offset_count = block_pair % STEPS
    val_block = (cond_block - offset_count) % blocks
    wave_val = lax.dynamic_slice_in_dim(valence, (val_block * NV_DEV).astype(jnp.int32), NV_DEV, 0).astype(jnp.float32)
    wave_cond = lax.dynamic_slice_in_dim(conduction, (cond_block * NC_DEV).astype(jnp.int32), NC_DEV, 0).astype(jnp.float32)
    energy_val = lax.dynamic_slice_in_dim(val_energy, (val_block * NV_DEV).astype(jnp.int32), NV_DEV, 0)
    energy_cond = lax.dynamic_slice_in_dim(cond_energy, (cond_block * NC_DEV).astype(jnp.int32), NC_DEV, 0)
    density = wave_val[:, None] * wave_cond[None, :]
    spectrum = jnp.fft.fftn(density, axes=(2, 3, 4)).reshape(NV_DEV, NC_DEV, NG ** 3)
    picked = jnp.take(spectrum, sphere_index, axis=2)
    weight = jnp.sqrt(4.0 / (energy_cond[None, :] - energy_val[:, None])) / NG ** 1.5
    panel_rows = jnp.stack([picked.real, picked.imag], axis=2) * weight[:, :, None, None]
    return panel_rows.reshape(NV_DEV * NC_DEV * 2, NPW).astype(jnp.bfloat16)

def reference(valence, conduction, val_energy, cond_energy, sphere_index):
    count = NV // NV_DEV * STEPS
    panels = lax.map(lambda block_pair: pair_rows(valence, conduction, val_energy, cond_energy, sphere_index, block_pair), jnp.arange(count, dtype=jnp.int32))
    stacked = panels.reshape(count * NV_DEV * NC_DEV * 2, NPW).astype(jnp.float32)
    gram = lax.dot_general(stacked, stacked, (((0,), (0,)), ((), ())), precision=lax.Precision.HIGHEST, preferred_element_type=jnp.float32)
    return gram * (-1.0 / math.sqrt(TOTAL_PAIRS))
```

```python
import functools
import math

import jax
import jax.numpy as jnp
import numpy as np
from jax import lax
from jax.experimental import pallas as pl
from jax.experimental.pallas import tpu as pltpu
from jax.sharding import PartitionSpec as P

GRID = 96
GMAX = 15
FOLD = 24


def split_table(values):
    high = np.asarray(values, np.float32).astype(jnp.bfloat16)
    low = (np.asarray(values, np.float64) - high.astype(np.float64)).astype(jnp.bfloat16)
    return high, low


def depth_table():
    angle = 2.0 * np.pi * (np.outer(np.arange(GRID), np.arange(16)) % GRID) / GRID
    rows = np.concatenate([np.cos(angle), -np.sin(angle)], axis=1)
    table = np.zeros((3, 128, 128))
    for third in range(3):
        table[third, :GRID, third * 32 : third * 32 + 32] = rows
        table[third, GRID:, 96:] = rows[third * 32 : third * 32 + 32]
    high, low = split_table(table.reshape(384, 128))
    wide = np.concatenate([high, low], axis=1)
    return np.concatenate([wide, wide], axis=0)


def height_table():
    freq = np.arange(32) - GMAX
    angle = 2.0 * np.pi * (np.outer(freq, np.arange(GRID)) % GRID) / GRID
    high, low = split_table(np.concatenate([np.cos(angle), np.sin(angle)], axis=0))
    return np.concatenate([np.concatenate([high, high], 1), np.concatenate([low, low], 1)], 0)


def width_table():
    angle = 2.0 * np.pi * (np.outer(np.arange(FOLD), np.arange(16)) % GRID) / GRID
    return np.concatenate([np.cos(angle), np.sin(angle)], axis=1).astype(np.float32)


def merge_table():
    table = np.zeros((4, 2, 2, 16, 2, 2, 4, 2, 16))
    for cls in range(4):
        for side in range(2):
            sign = 1 - 2 * side
            for cs in range(2):
                for cy in range(2):
                    for quarter in range(4):
                        for cz in range(2):
                            turns = -sign * cls * quarter - cy + cz
                            turns += -sign if cs else 0
                            value = (1, 1j, -1, -1j)[turns % 4]
                            for gz in range(16):
                                table[cls, 0, side, gz, cs, cy, quarter, cz, gz] = value.real if isinstance(value, complex) else value
                                table[cls, 1, side, gz, cs, cy, quarter, cz, gz] = value.imag if isinstance(value, complex) else 0
    table = table.reshape(4, 64, 512)
    return np.concatenate([table, table], axis=2).astype(jnp.bfloat16)


def pack_kernel(val_ref, cond_ref, val_out, cond_out):
    for source, target in ((val_ref, val_out), (cond_ref, cond_out)):
        extra = source[3].astype(jnp.float32)
        for third in range(3):
            main = source[third].astype(jnp.float32)
            piece = extra[:, :, third * 32 : third * 32 + 32]
            target[:, third] = jnp.concatenate([main, piece], axis=2).astype(jnp.bfloat16)


def packed(valence, conduction):
    step = 4
    shape = jax.ShapeDtypeStruct((FOLD, 3, GRID, 128), jnp.bfloat16)
    in_spec = pl.BlockSpec((4, step, GRID, GRID), lambda i: (0, i, 0, 0))
    out_spec = pl.BlockSpec((step, 3, GRID, 128), lambda i: (i, 0, 0, 0))
    view = (4, FOLD, GRID, GRID)
    return pl.pallas_call(
        pack_kernel,
        grid=(FOLD // step,),
        out_shape=(shape, shape),
        in_specs=[in_spec, in_spec],
        out_specs=(out_spec, out_spec),
        name="pack",
    )(valence.reshape(view), conduction.reshape(view))


def pair_kernel(
    first, steps, val_ref, cond_ref, weight_ref, width_ref, depth_ref, height_ref, merge_ref,
    out_ref, total
):
    step = pl.program_id(0)

    @pl.when(step == 0)
    def _():
        total[...] = jnp.zeros_like(total)

    density = val_ref[...].astype(jnp.float32) * cond_ref[...].astype(jnp.float32)
    high = density.astype(jnp.bfloat16)
    low = (density - high.astype(jnp.float32)).astype(jnp.bfloat16)
    columns = [part[:, third].reshape(2 * GRID, 128) for part in (high, low) for third in range(3)]
    deep = jnp.dot(
        jnp.concatenate(columns, axis=1), depth_ref[...], preferred_element_type=jnp.float32
    )
    deep = deep[:, :128] + deep[:, 128:]
    high = deep.astype(jnp.bfloat16)
    low = (deep - high.astype(jnp.float32)).astype(jnp.bfloat16)
    sides = [jnp.concatenate([high[s : s + GRID], low[s : s + GRID]], axis=0) for s in (0, GRID)]
    tall = jnp.dot(
        height_ref[...], jnp.concatenate(sides, axis=1), preferred_element_type=jnp.float32
    )
    tall = tall[:64] + tall[64:]
    here = first + 2 * step
    for cy in range(2):
        left = tall[cy * 32 : cy * 32 + 32, :128]
        right = tall[cy * 32 : cy * 32 + 32, 128:]
        for cs in range(2):
            for freq in range(cs, 16):
                entry = cs * 16 + freq
                total[freq % 4, cs, cy, freq // 4] += (
                    width_ref[here, entry] * left + width_ref[here + 1, entry] * right
                )

    @pl.when(step == steps - 1)
    def _():
        for cls in range(4):
            blocks = [
                total[cls, cs, cy].reshape(128, 128) for cs in range(2) for cy in range(2)
            ]
            full = jnp.concatenate(blocks, axis=1)
            top = full.astype(jnp.bfloat16)
            rest = (full - top.astype(jnp.float32)).astype(jnp.bfloat16)
            merged = lax.dot_general(
                merge_ref[cls],
                jnp.concatenate([top, rest], axis=1),
                (((1,), (1,)), ((), ())),
                preferred_element_type=jnp.float32,
            )
            out_ref[:, cls * 128 : cls * 128 + 128] = merged * weight_ref[0, 0]


def pair_cube(val, cond, weight, first, count):
    steps = count // 2
    data = pl.BlockSpec((2, 3, GRID, 128), lambda i: (i, 0, 0, 0))
    whole = pl.BlockSpec(memory_space=pltpu.VMEM)
    scalars = pl.BlockSpec(memory_space=pltpu.SMEM)
    return pl.pallas_call(
        functools.partial(pair_kernel, first, steps),
        grid=(steps,),
        out_shape=jax.ShapeDtypeStruct((64, 512), jnp.float32),
        in_specs=[data, data, scalars, scalars, whole, whole, whole],
        out_specs=pl.BlockSpec((64, 512), lambda i: (0, 0)),
        scratch_shapes=[pltpu.VMEM((4, 2, 2, 4, 32, 128), jnp.float32)],
        cost_estimate=pl.CostEstimate(
            flops=4_000_000_000, bytes_accessed=8_000_000, transcendentals=0
        ),
        name="pair_cube",
    )(val, cond, weight, width_table(), depth_table(), height_table(), merge_table())


def sphere_codes(sphere_index):
    def centred(values):
        return jnp.where(values > GRID // 2, values - GRID, values)

    gx = centred(sphere_index // (GRID * GRID))
    gy = centred(sphere_index // GRID % GRID)
    gz = centred(sphere_index % GRID)
    sign = jnp.where(gz < 0, -1, 1)
    gx, gy, gz = gx * sign, gy * sign, gz * sign
    size = jnp.abs(gx)
    cell = size % 4 * 128 + size // 4 * 32 + gy + GMAX
    lane = jnp.where(gx < 0, 16, 0) + gz
    return jnp.stack([cell, lane, sign]).reshape(3, 16, 1024).transpose(1, 0, 2)


def select_kernel(pairs, code_ref, cube_ref, out_ref, rows):
    cell = code_ref[0, 0:1, :]
    lane = code_ref[0, 1:2, :]
    sign = code_ref[0, 2:3, :].astype(jnp.float32)
    hot = (lax.broadcasted_iota(jnp.int32, (512, 1024), 0) == cell).astype(jnp.bfloat16)
    found = jnp.dot(cube_ref[...], hot, preferred_element_type=jnp.float32)
    keep = lax.broadcasted_iota(jnp.int32, (32, 1024), 0) == lane
    for pair in range(pairs):
        for part in range(2):
            entry = pair * 2 + part
            block = found[entry * 32 : entry * 32 + 32]
            picked = jnp.sum(jnp.where(keep, block, 0.0), axis=0, keepdims=True)
            if part == 1:
                picked = picked * sign
            for chunk in range(8):
                rows[chunk * 2 * pairs + entry, :] = picked[0, chunk * 128 : chunk * 128 + 128]
    out_ref[0] = rows[...].astype(jnp.bfloat16)


def select(cubes, codes):
    pairs = cubes.shape[0] // 64
    height = 16 * pairs
    return pl.pallas_call(
        functools.partial(select_kernel, pairs),
        grid=(16,),
        out_shape=jax.ShapeDtypeStruct((16, height, 128), jnp.bfloat16),
        in_specs=[
            pl.BlockSpec((1, 3, 1024), lambda i: (i, 0, 0)),
            pl.BlockSpec(memory_space=pltpu.VMEM),
        ],
        out_specs=pl.BlockSpec((1, height, 128), lambda i: (i, 0, 0)),
        scratch_shapes=[pltpu.VMEM((height, 128), jnp.float32)],
        name="select",
    )(codes, cubes)


def panel_product(panel, rows_axis, cols_axis):
    pair_count = panel.shape[0]
    plane_waves = panel.shape[1]
    row_width = plane_waves // rows_axis
    col_width = plane_waves // cols_axis
    wide_panel = lax.all_gather(panel, "col", axis=0, tiled=True)
    col_start = lax.axis_index("col") * col_width
    col_slice = lax.dynamic_slice_in_dim(wide_panel, col_start, col_width, 1)
    col_full = lax.all_gather(col_slice, "row", axis=0, tiled=True)
    row_full = lax.all_to_all(
        wide_panel.reshape(cols_axis * pair_count, plane_waves),
        "row",
        split_axis=1,
        concat_axis=0,
        tiled=True,
    )
    return lax.dot_general(
        row_full, col_full, (((0,), (0,)), ((), ())), preferred_element_type=jnp.float32
    )


def local(valence, conduction, val_energy, cond_energy, sphere_index):
    rows_axis = lax.axis_size("row")
    cols_axis = lax.axis_size("col")
    devices = rows_axis * cols_axis
    position = lax.axis_index(("row", "col"))
    codes = sphere_codes(sphere_index)
    val, cond = packed(valence, conduction)
    along = [(source, (source + 1) % devices) for source in range(devices)]
    passed = lax.ppermute(val, ("row", "col"), along)
    cubes = []
    for turn, held in enumerate((val, passed)):
        energy = lax.dynamic_slice_in_dim(val_energy, (position - turn) % devices, 1, 0)
        weight = jnp.sqrt(4.0 / (cond_energy - energy)) / GRID**1.5
        cubes.append(pair_cube(held, cond, weight.reshape(1, 1), 0, FOLD))
    pieces = select(jnp.concatenate(cubes).astype(jnp.bfloat16), codes)
    panel = pieces.reshape(16, 8, 4, 128).transpose(2, 0, 1, 3).reshape(4, 16384)
    product = panel_product(panel, rows_axis, cols_axis)
    return product * (-1.0 / math.sqrt(2 * devices))


def solution(mesh):
    placed = (
        P(("row", "col"), None, None, None),
        P(("row", "col"), None, None, None),
        P(),
        P(("row", "col")),
        P(),
    )
    return jax.shard_map(
        local, mesh=mesh, in_specs=placed, out_specs=P("row", "col"), check_vma=False
    )
```

```python
import functools
import math

import jax
import jax.numpy as jnp
import numpy as np
from jax import lax
from jax.experimental import pallas as pl
from jax.experimental.pallas import tpu as pltpu
from jax.sharding import PartitionSpec as P

GRID = 96
GMAX = 15
FOLD = 24


def split_table(values):
    high = np.asarray(values, np.float32).astype(jnp.bfloat16)
    low = (np.asarray(values, np.float64) - high.astype(np.float64)).astype(jnp.bfloat16)
    return high, low


def depth_table():
    angle = 2.0 * np.pi * (np.outer(np.arange(GRID), np.arange(16)) % GRID) / GRID
    rows = np.concatenate([np.cos(angle), -np.sin(angle)], axis=1)
    table = np.zeros((3, 128, 128))
    for third in range(3):
        table[third, :GRID, third * 32 : third * 32 + 32] = rows
        table[third, GRID:, 96:] = rows[third * 32 : third * 32 + 32]
    high, low = split_table(table.reshape(384, 128))
    wide = np.concatenate([high, low], axis=1)
    return np.concatenate([wide, wide], axis=0)


def height_table():
    freq = np.arange(32) - GMAX
    angle = 2.0 * np.pi * (np.outer(freq, np.arange(GRID)) % GRID) / GRID
    high, low = split_table(np.concatenate([np.cos(angle), np.sin(angle)], axis=0))
    return np.concatenate([np.concatenate([high, high], 1), np.concatenate([low, low], 1)], 0)


def width_table():
    angle = 2.0 * np.pi * (np.outer(np.arange(FOLD), np.arange(16)) % GRID) / GRID
    return np.concatenate([np.cos(angle), np.sin(angle)], axis=1).astype(np.float32)


def merge_table():
    table = np.zeros((4, 2, 2, 16, 2, 2, 4, 2, 16))
    for cls in range(4):
        for side in range(2):
            sign = 1 - 2 * side
            for cs in range(2):
                for cy in range(2):
                    for quarter in range(4):
                        for cz in range(2):
                            turns = -sign * cls * quarter - cy + cz
                            turns += -sign if cs else 0
                            value = (1, 1j, -1, -1j)[turns % 4]
                            for gz in range(16):
                                table[cls, 0, side, gz, cs, cy, quarter, cz, gz] = value.real if isinstance(value, complex) else value
                                table[cls, 1, side, gz, cs, cy, quarter, cz, gz] = value.imag if isinstance(value, complex) else 0
    table = table.reshape(4, 64, 512)
    return np.concatenate([table, table], axis=2).astype(jnp.bfloat16)


def pack_kernel(val_ref, cond_ref, val_out, cond_out):
    for source, target in ((val_ref, val_out), (cond_ref, cond_out)):
        extra = source[3].astype(jnp.float32)
        for third in range(3):
            main = source[third].astype(jnp.float32)
            piece = extra[:, :, third * 32 : third * 32 + 32]
            target[:, third] = jnp.concatenate([main, piece], axis=2).astype(jnp.bfloat16)


def packed(valence, conduction):
    step = 4
    shape = jax.ShapeDtypeStruct((FOLD, 3, GRID, 128), jnp.bfloat16)
    in_spec = pl.BlockSpec((4, step, GRID, GRID), lambda i: (0, i, 0, 0))
    out_spec = pl.BlockSpec((step, 3, GRID, 128), lambda i: (i, 0, 0, 0))
    view = (4, FOLD, GRID, GRID)
    return pl.pallas_call(
        pack_kernel,
        grid=(FOLD // step,),
        out_shape=(shape, shape),
        in_specs=[in_spec, in_spec],
        out_specs=(out_spec, out_spec),
        name="pack",
    )(valence.reshape(view), conduction.reshape(view))


def pair_kernel(
    first, steps, val_ref, cond_ref, weight_ref, width_ref, depth_ref, height_ref, merge_ref,
    out_ref, total
):
    step = pl.program_id(0)

    @pl.when(step == 0)
    def _():
        total[...] = jnp.zeros_like(total)

    density = val_ref[...].astype(jnp.float32) * cond_ref[...].astype(jnp.float32)
    high = density.astype(jnp.bfloat16)
    low = (density - high.astype(jnp.float32)).astype(jnp.bfloat16)
    columns = [part[:, third].reshape(2 * GRID, 128) for part in (high, low) for third in range(3)]
    deep = jnp.dot(
        jnp.concatenate(columns, axis=1), depth_ref[...], preferred_element_type=jnp.float32
    )
    deep = deep[:, :128] + deep[:, 128:]
    high = deep.astype(jnp.bfloat16)
    low = (deep - high.astype(jnp.float32)).astype(jnp.bfloat16)
    sides = [jnp.concatenate([high[s : s + GRID], low[s : s + GRID]], axis=0) for s in (0, GRID)]
    tall = jnp.dot(
        height_ref[...], jnp.concatenate(sides, axis=1), preferred_element_type=jnp.float32
    )
    tall = tall[:64] + tall[64:]
    here = first + 2 * step
    for cy in range(2):
        left = tall[cy * 32 : cy * 32 + 32, :128]
        right = tall[cy * 32 : cy * 32 + 32, 128:]
        for cs in range(2):
            for freq in range(cs, 16):
                entry = cs * 16 + freq
                total[freq % 4, cs, cy, freq // 4] += (
                    width_ref[here, entry] * left + width_ref[here + 1, entry] * right
                )

    @pl.when(step == steps - 1)
    def _():
        for cls in range(4):
            blocks = [
                total[cls, cs, cy].reshape(128, 128) for cs in range(2) for cy in range(2)
            ]
            full = jnp.concatenate(blocks, axis=1)
            top = full.astype(jnp.bfloat16)
            rest = (full - top.astype(jnp.float32)).astype(jnp.bfloat16)
            merged = lax.dot_general(
                merge_ref[cls],
                jnp.concatenate([top, rest], axis=1),
                (((1,), (1,)), ((), ())),
                preferred_element_type=jnp.float32,
            )
            out_ref[:, cls * 128 : cls * 128 + 128] = merged * weight_ref[0, 0]


def pair_cube(val, cond, weight, first, count):
    steps = count // 2
    data = pl.BlockSpec((2, 3, GRID, 128), lambda i: (i, 0, 0, 0))
    whole = pl.BlockSpec(memory_space=pltpu.VMEM)
    scalars = pl.BlockSpec(memory_space=pltpu.SMEM)
    return pl.pallas_call(
        functools.partial(pair_kernel, first, steps),
        grid=(steps,),
        out_shape=jax.ShapeDtypeStruct((64, 512), jnp.float32),
        in_specs=[data, data, scalars, scalars, whole, whole, whole],
        out_specs=pl.BlockSpec((64, 512), lambda i: (0, 0)),
        scratch_shapes=[pltpu.VMEM((4, 2, 2, 4, 32, 128), jnp.float32)],
        cost_estimate=pl.CostEstimate(
            flops=4_000_000_000, bytes_accessed=8_000_000, transcendentals=0
        ),
        name="pair_cube",
    )(val, cond, weight, width_table(), depth_table(), height_table(), merge_table())


def sphere_codes(sphere_index):
    def centred(values):
        return jnp.where(values > GRID // 2, values - GRID, values)

    gx = centred(sphere_index // (GRID * GRID))
    gy = centred(sphere_index // GRID % GRID)
    gz = centred(sphere_index % GRID)
    sign = jnp.where(gz < 0, -1, 1)
    gx, gy, gz = gx * sign, gy * sign, gz * sign
    size = jnp.abs(gx)
    cell = size % 4 * 128 + size // 4 * 32 + gy + GMAX
    lane = jnp.where(gx < 0, 16, 0) + gz
    return jnp.stack([cell, lane, sign]).reshape(3, 16, 1024).transpose(1, 0, 2)


def select_kernel(pairs, code_ref, cube_ref, out_ref, rows):
    cell = code_ref[0, 0:1, :]
    lane = code_ref[0, 1:2, :]
    sign = code_ref[0, 2:3, :].astype(jnp.float32)
    hot = (lax.broadcasted_iota(jnp.int32, (512, 1024), 0) == cell).astype(jnp.bfloat16)
    found = jnp.dot(cube_ref[...], hot, preferred_element_type=jnp.float32)
    keep = lax.broadcasted_iota(jnp.int32, (32, 1024), 0) == lane
    for pair in range(pairs):
        for part in range(2):
            entry = pair * 2 + part
            block = found[entry * 32 : entry * 32 + 32]
            picked = jnp.sum(jnp.where(keep, block, 0.0), axis=0, keepdims=True)
            if part == 1:
                picked = picked * sign
            for chunk in range(8):
                rows[chunk * 2 * pairs + entry, :] = picked[0, chunk * 128 : chunk * 128 + 128]
    out_ref[0] = rows[...].astype(jnp.bfloat16)


def select(cubes, codes):
    pairs = cubes.shape[0] // 64
    height = 16 * pairs
    return pl.pallas_call(
        functools.partial(select_kernel, pairs),
        grid=(16,),
        out_shape=jax.ShapeDtypeStruct((16, height, 128), jnp.bfloat16),
        in_specs=[
            pl.BlockSpec((1, 3, 1024), lambda i: (i, 0, 0)),
            pl.BlockSpec(memory_space=pltpu.VMEM),
        ],
        out_specs=pl.BlockSpec((1, height, 128), lambda i: (i, 0, 0)),
        scratch_shapes=[pltpu.VMEM((height, 128), jnp.float32)],
        name="select",
    )(codes, cubes)


ROWS = 16
COLS = 16
MESH = pl.DeviceIdType.MESH


def remote(source, target, send_sem, recv_sem, device):
    return pltpu.make_async_remote_copy(
        src_ref=source,
        dst_ref=target,
        send_sem=send_sem,
        recv_sem=recv_sem,
        device_id=device,
        device_id_type=MESH,
    )


def spread_kernel(
    pieces, row_out, col_out, row_in, col_in, wide, row_full, col_full,
    deal_send, deal_recv, row_send, row_recv, col_send, col_recv, out_sem
):
    row = lax.axis_index("row")
    col = lax.axis_index("col")
    barrier = pltpu.get_barrier_semaphore()
    for step in range(1, 16):
        for device in (((row + step) % ROWS, col), (row, (col + step) % COLS)):
            pl.semaphore_signal(barrier, inc=1, device_id=device, device_id_type=MESH)
    pl.semaphore_wait(barrier, 30)

    for step in range(1, 16):
        peer = (row + step) % ROWS
        remote(
            pieces.at[peer], row_in.at[row], deal_send.at[0], deal_recv.at[0], (peer, col)
        ).start()
    for step in range(1, 16):
        peer = (col + step) % COLS
        remote(
            pieces.at[peer], col_in.at[col], deal_send.at[1], deal_recv.at[1], (row, peer)
        ).start()
    row_in[pl.ds(row, 1)] = pieces[pl.ds(row, 1)]
    col_in[pl.ds(col, 1)] = pieces[pl.ds(col, 1)]

    def dealt(which, landing):
        return remote(
            pieces.at[pl.ds(0, 15)], landing.at[pl.ds(0, 15)],
            deal_send.at[which], deal_recv.at[which], (row, col)
        )

    def arrange(landing, full, slot):
        wide[...] = landing[...].astype(jnp.float32).reshape(512, 128)
        for chunk in range(8):
            for kind in range(4):
                lines = wide[pl.ds(chunk * 4 + kind, 16, stride=32), :]
                full[slot, kind * 16 : kind * 16 + 16, chunk * 128 : chunk * 128 + 128] = (
                    lines.astype(jnp.bfloat16)
                )

    sent = []

    def push(full, slot, device, send_sem, recv_sem):
        copy = remote(full.at[slot], full.at[slot], send_sem, recv_sem.at[slot], device)
        copy.start()
        sent.append(copy)

    def push_row(slot, device):
        push(row_full, slot, device, row_send.at[counts["row"]], row_recv)
        counts["row"] += 1

    def push_col(slot, device):
        push(col_full, slot, device, col_send.at[counts["col"]], col_recv)
        counts["col"] += 1

    def got_row(slot):
        remote(
            row_full.at[slot], row_full.at[slot], row_send.at[0], row_recv.at[slot], (row, col)
        ).wait_recv()

    def got_col(slot):
        remote(
            col_full.at[slot], col_full.at[slot], col_send.at[0], col_recv.at[slot], (row, col)
        ).wait_recv()

    counts = {"row": 0, "col": 0}

    high, depth = col // 8, col % 8
    near = (high * 8, (1 - high) * 8)

    def line(which, offset):
        return near[which] + (depth + offset + 8) % 8

    up, down = (row, line(0, 1)), (row, line(0, -1))
    across = (row, line(1, 0))
    x_at, y_at, core = row // 4, row % 4 // 2, row % 2

    def ring(which, offset, own_core=True):
        y_of = y_at if which == 0 else 1 - y_at
        core_of = core if own_core else 1 - core
        return (x_at + offset + 4) % 4 * 4 + y_of * 2 + core_of

    right, left = (ring(0, 1), col), (ring(0, -1), col)
    beside, mate = (ring(1, 0), col), (ring(0, 0, False), col)

    dealt(0, row_in).wait_recv()
    arrange(row_in, row_full, col)
    push_row(col, up)
    push_row(col, down)
    push_row(col, across)
    dealt(1, col_in).wait_recv()
    arrange(col_in, col_full, row)
    push_col(row, beside)
    push_col(row, right)
    push_col(row, left)
    push_col(row, mate)

    def col_step(which, offset, onward):
        slot = ring(which, offset)
        got_col(slot)
        for device in onward:
            push_col(slot, device)
        push_col(slot, mate)

    def row_step(which, offset, onward):
        slot = line(which, offset)
        got_row(slot)
        for device in onward:
            push_row(slot, device)

    col_step(1, 0, (right, left))
    row_step(0, -1, (up,))
    row_step(0, 1, (down,))
    col_step(0, -1, (right,))
    col_step(0, 1, ())
    row_step(1, 0, (up, down))
    col_step(1, 1, (left,))
    col_step(1, -1, ())
    row_step(0, -2, (up,))
    row_step(0, 2, (down,))
    col_step(0, -2, ())
    col_step(1, 2, ())
    row_step(1, -1, (up,))
    row_step(1, 1, (down,))
    row_step(0, -3, (up,))
    row_step(0, 3, ())
    for which in range(2):
        for offset in (0, -1, 1, 2):
            got_col(ring(which, offset, False))
    col_copy = pltpu.make_async_copy(col_full, col_out, out_sem.at[0])
    col_copy.start()
    row_step(1, -2, (up,))
    row_step(1, 2, (down,))
    row_step(1, 3, (down,))
    row_step(0, -4, ())
    row_step(1, -3, ())
    row_step(1, 4, ())
    row_copy = pltpu.make_async_copy(row_full, row_out, out_sem.at[1])
    row_copy.start()
    for which, landing in ((0, row_in), (1, col_in)):
        dealt(which, landing).wait_send()
    for copy in sent:
        copy.wait_send()
    col_copy.wait()
    row_copy.wait()


def spread(pieces):
    full = jax.ShapeDtypeStruct((16, 64, 1024), jnp.bfloat16)
    anywhere = pl.BlockSpec(memory_space=pl.ANY)
    dma = pltpu.SemaphoreType.DMA
    return pl.pallas_call(
        spread_kernel,
        out_shape=(full, full),
        in_specs=[pl.BlockSpec(memory_space=pltpu.VMEM)],
        out_specs=(anywhere, anywhere),
        scratch_shapes=[
            pltpu.VMEM((16, 32, 128), jnp.bfloat16),
            pltpu.VMEM((16, 32, 128), jnp.bfloat16),
            pltpu.VMEM((512, 128), jnp.float32),
            pltpu.VMEM((16, 64, 1024), jnp.bfloat16),
            pltpu.VMEM((16, 64, 1024), jnp.bfloat16),
            dma((2,)),
            dma((2,)),
            dma((15,)),
            dma((16,)),
            dma((15,)),
            dma((16,)),
            dma((2,)),
        ],
        compiler_params=pltpu.CompilerParams(
            collective_id=0, has_side_effects=True, vmem_limit_bytes=16 * 2**20
        ),
        name="spread",
    )(pieces)


def swap_table():
    table = np.zeros((16, 16, 16, 16), np.float32)
    for first in range(16):
        for second in range(16):
            table[first, second, second, first] = 1.0
    return table.reshape(256, 256).astype(jnp.bfloat16)


def gram_kernel(scale, row_ref, col_ref, swap_ref, out_ref, ordered):
    @pl.when(pl.program_id(0) == 0)
    def _():
        for kind in range(4):
            block = col_ref[:, kind * 16 : kind * 16 + 16, :].reshape(256, 1024)
            ordered[kind] = jnp.dot(
                swap_ref[...], block, preferred_element_type=jnp.float32
            ).astype(jnp.bfloat16)

    left = jnp.concatenate(
        [row_ref[:, kind * 16 : kind * 16 + 16, :].reshape(256, 256) for kind in range(4)], axis=0
    )
    out_ref[...] = scale * lax.dot_general(
        left,
        ordered[...].reshape(1024, 1024),
        (((0,), (0,)), ((), ())),
        preferred_element_type=jnp.float32,
    )


def gram(row_full, col_full, scale):
    return pl.pallas_call(
        functools.partial(gram_kernel, scale),
        grid=(4,),
        out_shape=jax.ShapeDtypeStruct((1024, 1024), jnp.float32),
        in_specs=[
            pl.BlockSpec((16, 64, 256), lambda i: (0, 0, i)),
            pl.BlockSpec((16, 64, 1024), lambda i: (0, 0, 0)),
            pl.BlockSpec(memory_space=pltpu.VMEM),
        ],
        out_specs=pl.BlockSpec((256, 1024), lambda i: (i, 0)),
        scratch_shapes=[pltpu.VMEM((4, 256, 1024), jnp.bfloat16)],
        compiler_params=pltpu.CompilerParams(vmem_limit_bytes=32 * 2**20),
        name="gram",
    )(row_full, col_full, swap_table())


def local(valence, conduction, val_energy, cond_energy, sphere_index):
    devices = lax.axis_size("row") * lax.axis_size("col")
    position = lax.axis_index(("row", "col"))
    codes = sphere_codes(sphere_index)
    val, cond = packed(valence, conduction)
    along = [(source, (source + 1) % devices) for source in range(devices)]
    passed = lax.ppermute(val, ("row", "col"), along)
    cubes = []
    for turn, held in enumerate((val, passed)):
        energy = lax.dynamic_slice_in_dim(val_energy, (position - turn) % devices, 1, 0)
        weight = jnp.sqrt(4.0 / (cond_energy - energy)) / GRID**1.5
        cubes.append(pair_cube(held, cond, weight.reshape(1, 1), 0, FOLD))
    pieces = select(jnp.concatenate(cubes).astype(jnp.bfloat16), codes)
    row_full, col_full = spread(pieces)
    return gram(row_full, col_full, -1.0 / math.sqrt(2 * devices))


def solution(mesh):
    placed = (
        P(("row", "col"), None, None, None),
        P(("row", "col"), None, None, None),
        P(),
        P(("row", "col")),
        P(),
    )
    return jax.shard_map(
        local, mesh=mesh, in_specs=placed, out_specs=P("row", "col"), check_vma=False
    )
```

```python
import functools
import math

import jax
import jax.numpy as jnp
import numpy as np
from jax import lax
from jax.experimental import pallas as pl
from jax.experimental.pallas import tpu as pltpu
from jax.sharding import PartitionSpec as P

GRID = 96
GMAX = 15
FOLD = 24
PART = 4
CHUNKS = 3
HALF = 12
ROWS = 16
COLS = 16
MESH = pl.DeviceIdType.MESH


def split_table(values):
    high = np.asarray(values, np.float32).astype(jnp.bfloat16)
    low = (np.asarray(values, np.float64) - high.astype(np.float64)).astype(jnp.bfloat16)
    return high, low


def depth_table():
    angle = 2.0 * np.pi * (np.outer(np.arange(GRID), np.arange(16)) % GRID) / GRID
    rows = np.concatenate([np.cos(angle), -np.sin(angle)], axis=1)
    table = np.zeros((3, 128, 128))
    for third in range(3):
        table[third, :GRID, third * 32 : third * 32 + 32] = rows
        table[third, GRID:, 96:] = rows[third * 32 : third * 32 + 32]
    high, low = split_table(table.reshape(384, 128))
    wide = np.concatenate([high, low], axis=1)
    return np.concatenate([wide, wide], axis=0)


def height_table():
    freq = np.arange(32) - GMAX
    angle = 2.0 * np.pi * (np.outer(freq, np.arange(GRID)) % GRID) / GRID
    high, low = split_table(np.concatenate([np.cos(angle), np.sin(angle)], axis=0))
    return np.concatenate([np.concatenate([high, high], 1), np.concatenate([low, low], 1)], 0)


def width_table():
    angle = 2.0 * np.pi * (np.outer(np.arange(FOLD), np.arange(16)) % GRID) / GRID
    return np.concatenate([np.cos(angle), np.sin(angle)], axis=1).astype(np.float32)


def merge_table():
    table = np.zeros((4, 2, 2, 16, 2, 2, 4, 2, 16))
    for cls in range(4):
        for side in range(2):
            sign = 1 - 2 * side
            for cs in range(2):
                for cy in range(2):
                    for quarter in range(4):
                        for cz in range(2):
                            turns = -sign * cls * quarter - cy + cz
                            turns += -sign if cs else 0
                            value = (1, 1j, -1, -1j)[turns % 4]
                            for gz in range(16):
                                table[cls, 0, side, gz, cs, cy, quarter, cz, gz] = value.real if isinstance(value, complex) else value
                                table[cls, 1, side, gz, cs, cy, quarter, cz, gz] = value.imag if isinstance(value, complex) else 0
    table = table.reshape(4, 64, 512)
    return np.concatenate([table, table], axis=2).astype(jnp.bfloat16)


def remote(source, target, send_sem, recv_sem, device):
    return pltpu.make_async_remote_copy(
        src_ref=source,
        dst_ref=target,
        send_sem=send_sem,
        recv_sem=recv_sem,
        device_id=device,
        device_id_type=MESH,
    )


def two_parts(values):
    high = values.astype(jnp.bfloat16)
    return high, (values - high.astype(jnp.float32)).astype(jnp.bfloat16)


def pack(raw, which, start, out):
    extra = raw[which, 3, start : start + PART].astype(jnp.float32)
    for third in range(3):
        main = raw[which, third, start : start + PART].astype(jnp.float32)
        piece = extra[:, :, third * 32 : third * 32 + 32]
        out[start : start + PART, third] = jnp.concatenate([main, piece], axis=2).astype(
            jnp.bfloat16
        )


def accumulate(val, cond, here, width, depth, height, total):
    density = val.astype(jnp.float32) * cond.astype(jnp.float32)
    columns = [
        part[:, third].reshape(PART * GRID, 128)
        for part in two_parts(density)
        for third in range(3)
    ]
    deep = jnp.dot(
        jnp.concatenate(columns, axis=1), depth[...], preferred_element_type=jnp.float32
    )
    high, low = two_parts(deep[:, :128] + deep[:, 128:])
    sides = [
        jnp.concatenate([high[s : s + GRID], low[s : s + GRID]], axis=0)
        for s in range(0, PART * GRID, GRID)
    ]
    tall = jnp.dot(
        height[...], jnp.concatenate(sides, axis=1), preferred_element_type=jnp.float32
    )
    tall = tall[:64] + tall[64:]
    for cy in range(2):
        parts = [
            tall[cy * 32 : cy * 32 + 32, 128 * near : 128 * near + 128] for near in range(PART)
        ]
        for cs in range(2):
            for freq in range(cs, 16):
                entry = cs * 16 + freq
                sums = total[freq % 4, cs, cy, freq // 4]
                for near in range(PART):
                    sums += width[here + near, entry] * parts[near]
                total[freq % 4, cs, cy, freq // 4] = sums


def merged(total, merge, out):
    for cls in range(4):
        full = jnp.concatenate(
            [total[cls, cs, cy].reshape(128, 128) for cs in range(2) for cy in range(2)], axis=1
        )
        out[:, cls * 128 : cls * 128 + 128] = lax.dot_general(
            merge[cls],
            jnp.concatenate(two_parts(full), axis=1),
            (((1,), (1,)), ((), ())),
            preferred_element_type=jnp.float32,
        )


def sphere_codes(sphere, cells, lanes, signs):
    index = sphere[...]
    upper = ((index >> 5) * 43691) >> 17
    x_part = ((index >> 10) * 7282) >> 16

    def centred(values):
        return jnp.where(values > GRID // 2, values - GRID, values)

    gx = centred(x_part)
    gy = centred(upper - GRID * x_part)
    gz = centred(index - GRID * upper)
    sign = jnp.where(gz < 0, -1, 1)
    gx, gy, gz = gx * sign, gy * sign, gz * sign
    size = jnp.abs(gx)
    cell = (size & 3) * 128 + (size >> 2) * 32 + gy + GMAX
    cells[...] = (cell & 255).astype(jnp.float32)
    lanes[...] = (cell >> 8) * 32 + jnp.where(gx < 0, 16, 0) + gz
    signs[...] = sign.astype(jnp.float32)


def fill_table(cube, weight, table):
    for part in range(2):
        for half in range(2):
            start = part * 64 + half * 32
            block = cube[part * 32 : part * 32 + 32, half * 256 : half * 256 + 256]
            table[start : start + 32, :] = (block * weight).astype(jnp.bfloat16)


def select_block(block, table, cells, lanes, signs, stack, out):
    start = pl.multiple_of(block * 8, 8)
    cell = cells[pl.ds(start, 8), :].astype(jnp.bfloat16)
    lane = lanes[pl.ds(start, 8), :]
    sign = signs[pl.ds(start, 8), :]
    count = lax.broadcasted_iota(jnp.int32, (256, 128), 0).astype(jnp.float32).astype(jnp.bfloat16)
    one, zero = jnp.bfloat16(1), jnp.bfloat16(0)
    hot = [jnp.where(count == cell[c : c + 1, :], one, zero) for c in range(8)]
    found = jnp.dot(
        table[...], jnp.concatenate(hot, axis=1), preferred_element_type=jnp.float32
    )
    deep = lax.broadcasted_iota(jnp.int32, (64, 128), 0)
    for c in range(8):
        keep = deep == lane[c : c + 1, :]
        for part in range(2):
            mask = jnp.where(keep, sign[c : c + 1, :] if part else 1.0, 0.0)
            values = found[part * 64 : part * 64 + 64, c * 128 : c * 128 + 128] * mask
            entry = c * 2 + part
            stack[entry * 8 : entry * 8 + 8, :] = jnp.sum(values.reshape(8, 8, 128), axis=0)
    groups = lax.broadcasted_iota(jnp.int32, (16, 128), 1) >> 3
    adder = (groups == lax.broadcasted_iota(jnp.int32, (16, 128), 0)).astype(jnp.bfloat16)
    out[block] = jnp.dot(
        adder, stack[...].astype(jnp.bfloat16), preferred_element_type=jnp.float32
    ).astype(jnp.bfloat16)


def arrange(landing, wide, full, slot):
    wide[...] = landing[...].astype(jnp.float32).reshape(256, 128)
    for chunk in range(8):
        for kind in range(2):
            lines = wide[pl.ds(chunk * 2 + kind, 16, stride=16), :]
            full[slot, kind * 16 : kind * 16 + 16, chunk * 128 : chunk * 128 + 128] = (
                lines.astype(jnp.bfloat16)
            )


def panel_kernel(
    val_hbm, cond_hbm, val_energy, cond_energy, sphere, width, depth_hbm, height_hbm, merge_hbm,
    row_out, col_out,
    raw, val, cond, got_val, got_cond, depth, height, merge, total, cube, cube_sent, cube_got,
    cells, lanes, signs, table, stack, pieces, row_in, col_in, wide, row_full, col_full,
    load_sem, table_sem, shift_send, shift_recv, cube_sem, deal_send, deal_recv,
    row_send, row_recv, col_send, col_recv, out_sem
):
    row = lax.axis_index("row")
    col = lax.axis_index("col")
    here = row * COLS + col
    after = (here + 1) % (ROWS * COLS)
    before = (here + ROWS * COLS - 1) % (ROWS * COLS)
    next_device = (after // COLS, after % COLS)
    last_device = (before // COLS, before % COLS)

    loads = {}
    for chunk in range(CHUNKS):
        for which, source, start in (
            (0, val_hbm, chunk * PART), (1, cond_hbm, HALF + chunk * PART),
        ):
            loads[which, start] = (source, len(loads))
    for chunk in range(CHUNKS):
        for which, source, start in (
            (0, val_hbm, HALF + chunk * PART), (1, cond_hbm, chunk * PART),
        ):
            loads[which, start] = (source, len(loads))

    def load(which, start):
        source, number = loads[which, start]
        window = pl.ds(start, PART)
        return pltpu.make_async_copy(
            source.at[:, window], raw.at[which, :, window], load_sem.at[number]
        )

    for which, start in loads:
        load(which, start).start()
    constants = [
        pltpu.make_async_copy(source, target, table_sem.at[number])
        for number, (source, target) in enumerate(
            ((depth_hbm, depth), (height_hbm, height), (merge_hbm, merge))
        )
    ]
    for copy in constants:
        copy.start()

    barrier = pltpu.get_barrier_semaphore()
    for step in range(1, 16):
        for device in (((row + step) % ROWS, col), (row, (col + step) % COLS)):
            pl.semaphore_signal(barrier, inc=1, device_id=device, device_id_type=MESH)
    for device in (next_device, last_device):
        pl.semaphore_signal(barrier, inc=1, device_id=device, device_id_type=MESH)
    sphere_codes(sphere, cells, lanes, signs)
    pl.semaphore_wait(barrier, 32)

    def val_shift(chunk):
        window = pl.ds(chunk * PART, PART)
        return remote(
            val.at[window], got_val.at[window],
            shift_send.at[0, chunk], shift_recv.at[0, chunk], next_device
        )

    def cond_shift(chunk):
        return remote(
            cond.at[pl.ds(HALF + chunk * PART, PART)], got_cond.at[pl.ds(chunk * PART, PART)],
            shift_send.at[1, chunk], shift_recv.at[1, chunk], last_device
        )

    for chunk in range(CHUNKS):
        load(0, chunk * PART).wait()
        pack(raw, 0, chunk * PART, val)
        val_shift(chunk).start()
        load(1, HALF + chunk * PART).wait()
        pack(raw, 1, HALF + chunk * PART, cond)
        cond_shift(chunk).start()
    for chunk in range(CHUNKS):
        load(0, HALF + chunk * PART).wait()
        pack(raw, 0, HALF + chunk * PART, val)
        load(1, chunk * PART).wait()
        pack(raw, 1, chunk * PART, cond)
    for copy in constants:
        copy.wait()

    def pair_weight(position):
        gap = jnp.full((8, 128), cond_energy[0] - val_energy[position], jnp.float32)
        return (jnp.sqrt(4.0 / gap) * (1.0 / GRID**1.5))[0:1, 0:1]

    def add_part(val_ref, val_at, cond_ref, cond_at, first, which):
        accumulate(
            val_ref[pl.ds(val_at, PART)], cond_ref[pl.ds(cond_at, PART)], first,
            width, depth, height, total.at[which]
        )

    high, low = col // 8, col % 8
    near = (high * 8, (1 - high) * 8)
    x_at, y_at, core = row // 4, row % 4 // 2, row % 2

    def line(which, offset):
        return near[which] + (low + offset + 8) % 8

    def ring(which, offset, own_core=True):
        y_of = y_at if which == 0 else 1 - y_at
        core_of = core if own_core else 1 - core
        return (x_at + offset + 4) % 4 * 4 + y_of * 2 + core_of

    up, down, across = (row, line(0, 1)), (row, line(0, -1)), (row, line(1, 0))
    right, left = (ring(0, 1), col), (ring(0, -1), col)
    beside, mate = (ring(1, 0), col), (ring(0, 0, False), col)
    sent = []

    def deal(turn):
        def one(step):
            block = (row + step) % ROWS
            select_block(block, table, cells, lanes, signs, stack, pieces.at[turn])

            @pl.when(block != row)
            def _():
                remote(
                    pieces.at[turn, block], row_in.at[turn, row],
                    deal_send.at[turn, 0], deal_recv.at[turn, 0], (block, col)
                ).start()

            @pl.when(block != col)
            def _():
                remote(
                    pieces.at[turn, block], col_in.at[turn, col],
                    deal_send.at[turn, 1], deal_recv.at[turn, 1], (row, block)
                ).start()

        pl.loop(0, 16)(one)
        row_in[turn, pl.ds(row, 1)] = pieces[turn, pl.ds(row, 1)]
        col_in[turn, pl.ds(col, 1)] = pieces[turn, pl.ds(col, 1)]

    def dealt(turn, which):
        landing = (row_in, col_in)[which]
        return remote(
            pieces.at[turn, pl.ds(0, 15)], landing.at[turn, pl.ds(0, 15)],
            deal_send.at[turn, which], deal_recv.at[turn, which], (row, col)
        )

    def spread(turn):
        counts = [0, 0]
        fulls = (row_full.at[turn], col_full.at[turn])
        sends = (row_send.at[turn], col_send.at[turn])
        recvs = (row_recv.at[turn], col_recv.at[turn])

        def push(which, slot, device):
            full = fulls[which]
            copy = remote(
                full.at[slot], full.at[slot], sends[which].at[counts[which]],
                recvs[which].at[slot], device
            )
            counts[which] += 1
            copy.start()
            sent.append(copy)

        def got(which, slot):
            full = fulls[which]
            remote(
                full.at[slot], full.at[slot], sends[which].at[0], recvs[which].at[slot], (row, col)
            ).wait_recv()

        def row_step(which, offset, *onward):
            slot = line(which, offset)
            got(0, slot)
            for device in onward:
                push(0, slot, device)

        def col_step(which, offset, *onward):
            slot = ring(which, offset)
            got(1, slot)
            for device in onward:
                push(1, slot, device)
            push(1, slot, mate)

        dealt(turn, 0).wait_recv()
        arrange(row_in.at[turn], wide, row_full.at[turn], col)
        push(0, col, up)
        push(0, col, down)
        push(0, col, across)
        yield
        dealt(turn, 1).wait_recv()
        arrange(col_in.at[turn], wide, col_full.at[turn], row)
        push(1, row, beside)
        push(1, row, right)
        push(1, row, left)
        push(1, row, mate)
        yield
        col_step(1, 0, right, left)
        row_step(0, -1, up)
        row_step(0, 1, down)
        row_step(1, 0, up, down)
        yield
        col_step(0, -1, right)
        col_step(0, 1)
        row_step(0, -2, up)
        row_step(0, 2, down)
        yield
        col_step(1, 1, left)
        col_step(1, -1)
        row_step(1, -1, up)
        row_step(1, 1, down)
        yield
        col_step(0, -2)
        col_step(1, 2)
        row_step(0, -3, up)
        row_step(0, 3)
        yield
        for which in range(2):
            for offset in (0, -1, 1, 2):
                got(1, ring(which, offset, False))
        col_copy = pltpu.make_async_copy(col_full.at[turn], col_out.at[turn], out_sem.at[turn, 1])
        col_copy.start()
        row_step(1, -2, up)
        row_step(1, 2, down)
        row_step(1, 3, down)
        yield
        row_step(0, -4)
        row_step(1, -3)
        row_step(1, 4)
        row_copy = pltpu.make_async_copy(row_full.at[turn], row_out.at[turn], out_sem.at[turn, 0])
        row_copy.start()
        yield
        col_copy.wait()
        row_copy.wait()

    total[...] = jnp.zeros_like(total)

    @pl.loop(0, FOLD // PART)
    def _(step):
        at = step * PART
        add_part(val, at, cond, at, at, 0)

    merged(total.at[0], merge, cube)
    total[0] = jnp.zeros_like(total[0])
    fill_table(cube, pair_weight(here), table)
    deal(0)
    early = spread(0)

    def shifted(chunk):
        at = chunk * PART
        cond_shift(chunk).wait_recv()
        add_part(val, HALF + at, got_cond, at, HALF + at, 0)
        if chunk == CHUNKS - 1:
            merged(total.at[0], merge, cube_sent)
            cube_copy.start()
        val_shift(chunk).wait_recv()
        add_part(got_val, at, cond, at, at, 1)

    cube_copy = remote(cube_sent, cube_got, cube_sem.at[0], cube_sem.at[1], next_device)
    shifted(0)
    next(early)
    next(early)
    shifted(1)
    next(early)
    next(early)
    shifted(2)
    merged(total.at[1], merge, cube)
    next(early)
    cube_copy.wait_recv()
    cube[...] += cube_got[...]
    fill_table(cube, pair_weight(before), table)
    deal(1)
    next(early)
    late = spread(1)
    next(late)
    next(late)
    next(early)
    next(late)
    next(early)
    for stage in late:
        pass
    for stage in early:
        pass
    for turn in range(2):
        for which in range(2):
            dealt(turn, which).wait_send()
    for chunk in range(CHUNKS):
        val_shift(chunk).wait_send()
        cond_shift(chunk).wait_send()
    cube_copy.wait_send()
    for copy in sent:
        copy.wait_send()


def panels(valence, conduction, val_energy, cond_energy, sphere_index):
    full = jax.ShapeDtypeStruct((2, 16, 32, 1024), jnp.bfloat16)
    anywhere = pl.BlockSpec(memory_space=pl.ANY)
    scalars = pl.BlockSpec(memory_space=pltpu.SMEM)
    dma = pltpu.SemaphoreType.DMA
    f32, bf16 = jnp.float32, jnp.bfloat16
    view = (4, FOLD, GRID, GRID)
    return pl.pallas_call(
        panel_kernel,
        out_shape=(full, full),
        in_specs=[
            anywhere, anywhere, scalars, scalars, pl.BlockSpec(memory_space=pltpu.VMEM), scalars,
            anywhere, anywhere, anywhere,
        ],
        out_specs=(anywhere, anywhere),
        scratch_shapes=[
            pltpu.VMEM((2, 4, FOLD, GRID, GRID), bf16),
            pltpu.VMEM((FOLD, 3, GRID, 128), bf16),
            pltpu.VMEM((FOLD, 3, GRID, 128), bf16),
            pltpu.VMEM((HALF, 3, GRID, 128), bf16),
            pltpu.VMEM((HALF, 3, GRID, 128), bf16),
            pltpu.VMEM((768, 256), bf16),
            pltpu.VMEM((128, 192), bf16),
            pltpu.VMEM((4, 64, 1024), bf16),
            pltpu.VMEM((2, 4, 2, 2, 4, 32, 128), f32),
            pltpu.VMEM((64, 512), f32),
            pltpu.VMEM((64, 512), f32),
            pltpu.VMEM((64, 512), f32),
            pltpu.VMEM((128, 128), f32),
            pltpu.VMEM((128, 128), jnp.int32),
            pltpu.VMEM((128, 128), f32),
            pltpu.VMEM((128, 256), bf16),
            pltpu.VMEM((128, 128), f32),
            pltpu.VMEM((2, 16, 16, 128), bf16),
            pltpu.VMEM((2, 16, 16, 128), bf16),
            pltpu.VMEM((2, 16, 16, 128), bf16),
            pltpu.VMEM((256, 128), f32),
            pltpu.VMEM((2, 16, 32, 1024), bf16),
            pltpu.VMEM((2, 16, 32, 1024), bf16),
            dma((4 * CHUNKS,)),
            dma((3,)),
            dma((2, CHUNKS)),
            dma((2, CHUNKS)),
            dma((2,)),
            dma((2, 2)),
            dma((2, 2)),
            dma((2, 15)),
            dma((2, 16)),
            dma((2, 15)),
            dma((2, 16)),
            dma((2, 2)),
        ],
        compiler_params=pltpu.CompilerParams(
            collective_id=0, has_side_effects=True, vmem_limit_bytes=60 * 2**20
        ),
        name="panels",
    )(
        valence.reshape(view), conduction.reshape(view), val_energy, cond_energy,
        sphere_index.reshape(128, 128), width_table(), depth_table(), height_table(), merge_table(),
    )


def swap_table():
    table = np.zeros((16, 16, 16, 16), np.float32)
    for first in range(16):
        for second in range(16):
            table[first, second, second, first] = 1.0
    return table.reshape(256, 256).astype(jnp.bfloat16)


def gram_kernel(scale, row_ref, col_ref, swap_ref, out_ref, ordered):
    @pl.when(pl.program_id(0) == 0)
    def _():
        for turn in range(2):
            for kind in range(2):
                block = col_ref[turn, :, kind * 16 : kind * 16 + 16, :].reshape(256, 1024)
                ordered[turn * 2 + kind] = jnp.dot(
                    swap_ref[...], block, preferred_element_type=jnp.float32
                ).astype(jnp.bfloat16)

    left = [
        row_ref[turn, :, kind * 16 : kind * 16 + 16, :].reshape(256, 256)
        for turn in range(2)
        for kind in range(2)
    ]
    out_ref[...] = scale * lax.dot_general(
        jnp.concatenate(left, axis=0),
        ordered[...].reshape(1024, 1024),
        (((0,), (0,)), ((), ())),
        preferred_element_type=jnp.float32,
    )


def gram(row_full, col_full, scale):
    return pl.pallas_call(
        functools.partial(gram_kernel, scale),
        grid=(4,),
        out_shape=jax.ShapeDtypeStruct((1024, 1024), jnp.float32),
        in_specs=[
            pl.BlockSpec((2, 16, 32, 256), lambda i: (0, 0, 0, i)),
            pl.BlockSpec((2, 16, 32, 1024), lambda i: (0, 0, 0, 0)),
            pl.BlockSpec(memory_space=pltpu.VMEM),
        ],
        out_specs=pl.BlockSpec((256, 1024), lambda i: (i, 0)),
        scratch_shapes=[pltpu.VMEM((4, 256, 1024), jnp.bfloat16)],
        compiler_params=pltpu.CompilerParams(vmem_limit_bytes=60 * 2**20),
        name="gram",
    )(row_full, col_full, swap_table())


def local(valence, conduction, val_energy, cond_energy, sphere_index):
    devices = lax.axis_size("row") * lax.axis_size("col")
    row_full, col_full = panels(valence, conduction, val_energy, cond_energy, sphere_index)
    return gram(row_full, col_full, -1.0 / math.sqrt(2 * devices))


def solution(mesh):
    placed = (
        P(("row", "col"), None, None, None),
        P(("row", "col"), None, None, None),
        P(),
        P(("row", "col")),
        P(),
    )
    return jax.shard_map(
        local, mesh=mesh, in_specs=placed, out_specs=P("row", "col"), check_vma=False
    )
```

```python
import functools
import math

import jax
import jax.numpy as jnp
import numpy as np
from jax import lax
from jax.experimental import pallas as pl
from jax.experimental.pallas import tpu as pltpu
from jax.sharding import PartitionSpec as P

GRID = 96
GMAX = 15
FOLD = 24
PART = 4
CHUNKS = 3
HALF = 12
WIDE_PART = 8
GROUP = 4
ROWS = 16
COLS = 16
MESH = pl.DeviceIdType.MESH


def split_table(values):
    high = np.asarray(values, np.float32).astype(jnp.bfloat16)
    low = (np.asarray(values, np.float64) - high.astype(np.float64)).astype(jnp.bfloat16)
    return high, low


def depth_table():
    angle = 2.0 * np.pi * (np.outer(np.arange(GRID), np.arange(16)) % GRID) / GRID
    rows = np.concatenate([np.cos(angle), -np.sin(angle)], axis=1)
    table = np.zeros((3, 128, 128))
    for third in range(3):
        table[third, :GRID, third * 32 : third * 32 + 32] = rows
        table[third, GRID:, 96:] = rows[third * 32 : third * 32 + 32]
    high, low = split_table(table.reshape(384, 128))
    wide = np.concatenate([high, low], axis=1)
    return np.concatenate([wide, wide], axis=0)


def height_table():
    freq = np.arange(32) - GMAX
    angle = 2.0 * np.pi * (np.outer(freq, np.arange(GRID)) % GRID) / GRID
    high, low = split_table(np.concatenate([np.cos(angle), np.sin(angle)], axis=0))
    return np.concatenate([np.concatenate([high, high], 1), np.concatenate([low, low], 1)], 0)


def width_table():
    angle = 2.0 * np.pi * (np.outer(np.arange(FOLD), np.arange(16)) % GRID) / GRID
    return np.concatenate([np.cos(angle), np.sin(angle)], axis=1).astype(np.float32)


def merge_table():
    table = np.zeros((4, 2, 2, 16, 2, 2, 4, 2, 16))
    for cls in range(4):
        for side in range(2):
            sign = 1 - 2 * side
            for cs in range(2):
                for cy in range(2):
                    for quarter in range(4):
                        for cz in range(2):
                            turns = -sign * cls * quarter - cy + cz
                            turns += -sign if cs else 0
                            value = (1, 1j, -1, -1j)[turns % 4]
                            for gz in range(16):
                                table[cls, 0, side, gz, cs, cy, quarter, cz, gz] = value.real if isinstance(value, complex) else value
                                table[cls, 1, side, gz, cs, cy, quarter, cz, gz] = value.imag if isinstance(value, complex) else 0
    table = table.reshape(4, 64, 512)
    return np.concatenate([table, table], axis=2).astype(jnp.bfloat16)


def swap_table():
    table = np.zeros((16, 16, 16, 16), np.float32)
    for first in range(16):
        for second in range(16):
            table[first, second, second, first] = 1.0
    return table.reshape(256, 256).astype(jnp.bfloat16)


def remote(source, target, send_sem, recv_sem, device):
    return pltpu.make_async_remote_copy(
        src_ref=source,
        dst_ref=target,
        send_sem=send_sem,
        recv_sem=recv_sem,
        device_id=device,
        device_id_type=MESH,
    )


def two_parts(values):
    high = values.astype(jnp.bfloat16)
    return high, (values - high.astype(jnp.float32)).astype(jnp.bfloat16)


def pack(raw, which, start, out):
    extra = raw[which, 3, start : start + PART].astype(jnp.float32)
    for third in range(3):
        main = raw[which, third, start : start + PART].astype(jnp.float32)
        piece = extra[:, :, third * 32 : third * 32 + 32]
        out[start : start + PART, third] = jnp.concatenate([main, piece], axis=2).astype(
            jnp.bfloat16
        )


def accumulate(val, cond, here, width, depth, height, total):
    size = val.shape[0]
    density = val.astype(jnp.float32) * cond.astype(jnp.float32)
    columns = [
        part[:, third].reshape(size * GRID, 128)
        for part in two_parts(density)
        for third in range(3)
    ]
    deep = jnp.dot(
        jnp.concatenate(columns, axis=1), depth[...], preferred_element_type=jnp.float32
    )
    high, low = two_parts(deep[:, :128] + deep[:, 128:])
    sides = [
        jnp.concatenate([high[s : s + GRID], low[s : s + GRID]], axis=0)
        for s in range(0, size * GRID, GRID)
    ]
    tall = jnp.dot(
        height[...], jnp.concatenate(sides, axis=1), preferred_element_type=jnp.float32
    )
    tall = tall[:64] + tall[64:]
    for cy in range(2):
        parts = [
            tall[cy * 32 : cy * 32 + 32, 128 * near : 128 * near + 128] for near in range(size)
        ]
        for cs in range(2):
            for freq in range(cs, 16):
                entry = cs * 16 + freq
                sums = total[freq % 4, cs, cy, freq // 4]
                for near in range(size):
                    sums += width[here + near, entry] * parts[near]
                total[freq % 4, cs, cy, freq // 4] = sums


def merged(total, merge, out):
    for cls in range(4):
        full = jnp.concatenate(
            [total[cls, cs, cy].reshape(128, 128) for cs in range(2) for cy in range(2)], axis=1
        )
        out[:, cls * 128 : cls * 128 + 128] = lax.dot_general(
            merge[cls],
            jnp.concatenate(two_parts(full), axis=1),
            (((1,), (1,)), ((), ())),
            preferred_element_type=jnp.float32,
        )


def sphere_codes(sphere, cells, lanes, signs):
    index = sphere[...]
    upper = ((index >> 5) * 43691) >> 17
    x_part = ((index >> 10) * 7282) >> 16

    def centred(values):
        return jnp.where(values > GRID // 2, values - GRID, values)

    gx = centred(x_part)
    gy = centred(upper - GRID * x_part)
    gz = centred(index - GRID * upper)
    sign = jnp.where(gz < 0, -1, 1)
    gx, gy, gz = gx * sign, gy * sign, gz * sign
    size = jnp.abs(gx)
    cell = (size & 3) * 128 + (size >> 2) * 32 + gy + GMAX
    cells[...] = (cell & 255).astype(jnp.float32)
    lanes[...] = (cell >> 8) * 32 + jnp.where(gx < 0, 16, 0) + gz
    signs[...] = sign.astype(jnp.float32)


def fill_table(cube, weight, table):
    for part in range(2):
        for half in range(2):
            start = part * 64 + half * 32
            block = cube[part * 32 : part * 32 + 32, half * 256 : half * 256 + 256]
            table[start : start + 32, :] = (block * weight).astype(jnp.bfloat16)


def select_group(first, table, cells, lanes, signs, out):
    start = pl.multiple_of(first * 8, 8)
    cell = cells[pl.ds(start, GROUP * 8), :].astype(jnp.bfloat16)
    lane = lanes[pl.ds(start, GROUP * 8), :]
    sign = signs[pl.ds(start, GROUP * 8), :]
    count = lax.broadcasted_iota(jnp.int32, (256, 128), 0).astype(jnp.float32).astype(jnp.bfloat16)
    one, zero = jnp.bfloat16(1), jnp.bfloat16(0)
    hot = [jnp.where(count == cell[c : c + 1, :], one, zero) for c in range(GROUP * 8)]
    found = jnp.dot(
        table[...], jnp.concatenate(hot, axis=1), preferred_element_type=jnp.float32
    )
    deep = lax.broadcasted_iota(jnp.int32, (64, 128), 0)
    groups = lax.broadcasted_iota(jnp.int32, (16, 128), 1) >> 3
    adder = (groups == lax.broadcasted_iota(jnp.int32, (16, 128), 0)).astype(jnp.bfloat16)
    for block in range(GROUP):
        parts = []
        for c in range(block * 8, block * 8 + 8):
            keep = deep == lane[c : c + 1, :]
            for part in range(2):
                mask = jnp.where(keep, sign[c : c + 1, :] if part else 1.0, 0.0)
                values = found[part * 64 : part * 64 + 64, c * 128 : c * 128 + 128] * mask
                parts.append(jnp.sum(values.reshape(8, 8, 128), axis=0))
        stacked = jnp.concatenate(parts, axis=0).astype(jnp.bfloat16)
        out[first + block] = jnp.dot(
            adder, stacked, preferred_element_type=jnp.float32
        ).astype(jnp.bfloat16)


def arrange(landing, wide, full, slot):
    wide[...] = landing[...].astype(jnp.float32).reshape(256, 128)
    for chunk in range(8):
        for kind in range(2):
            lines = wide[pl.ds(chunk * 2 + kind, 16, stride=16), :]
            full[slot, kind * 16 : kind * 16 + 16, chunk * 128 : chunk * 128 + 128] = (
                lines.astype(jnp.bfloat16)
            )


def panel_kernel(
    scale, val_hbm, cond_hbm, val_energy, cond_energy, sphere, width, depth_hbm, height_hbm, merge_hbm,
    swap_hbm, gram,
    raw, val, cond, got_val, got_cond, depth, height, merge, swap, total, cube, cube_sent, cube_got,
    cells, lanes, signs, table, pieces, row_in, col_in, wide, row_full, col_full,
    ordered, load_sem, table_sem, shift_send, shift_recv, cube_sem, deal_send, deal_recv,
    row_send, row_recv, col_send, col_recv
):
    row = lax.axis_index("row")
    col = lax.axis_index("col")
    here = row * COLS + col
    after = (here + 1) % (ROWS * COLS)
    before = (here + ROWS * COLS - 1) % (ROWS * COLS)
    next_device = (after // COLS, after % COLS)
    last_device = (before // COLS, before % COLS)

    loads = {}
    for chunk in range(CHUNKS):
        for which, source, start in (
            (0, val_hbm, chunk * PART), (1, cond_hbm, HALF + chunk * PART),
        ):
            loads[which, start] = (source, len(loads))
    for chunk in range(CHUNKS):
        for which, source, start in (
            (0, val_hbm, HALF + chunk * PART), (1, cond_hbm, chunk * PART),
        ):
            loads[which, start] = (source, len(loads))

    def load(which, start):
        source, number = loads[which, start]
        window = pl.ds(start, PART)
        return pltpu.make_async_copy(
            source.at[:, window], raw.at[which, :, window], load_sem.at[number]
        )

    for which, start in loads:
        load(which, start).start()
    constants = [
        pltpu.make_async_copy(source, target, table_sem.at[number])
        for number, (source, target) in enumerate(
            ((depth_hbm, depth), (height_hbm, height), (merge_hbm, merge), (swap_hbm, swap))
        )
    ]
    for copy in constants:
        copy.start()

    barrier = pltpu.get_barrier_semaphore()
    for step in range(1, 16):
        for device in (((row + step) % ROWS, col), (row, (col + step) % COLS)):
            pl.semaphore_signal(barrier, inc=1, device_id=device, device_id_type=MESH)
    for device in (next_device, last_device):
        pl.semaphore_signal(barrier, inc=1, device_id=device, device_id_type=MESH)
    sphere_codes(sphere, cells, lanes, signs)
    pl.semaphore_wait(barrier, 32)

    def val_shift(chunk):
        window = pl.ds(chunk * PART, PART)
        return remote(
            val.at[window], got_val.at[window],
            shift_send.at[0, chunk], shift_recv.at[0, chunk], next_device
        )

    def cond_shift(chunk):
        return remote(
            cond.at[pl.ds(HALF + chunk * PART, PART)], got_cond.at[pl.ds(chunk * PART, PART)],
            shift_send.at[1, chunk], shift_recv.at[1, chunk], last_device
        )

    for chunk in range(CHUNKS):
        load(0, chunk * PART).wait()
        pack(raw, 0, chunk * PART, val)
        val_shift(chunk).start()
        load(1, HALF + chunk * PART).wait()
        pack(raw, 1, HALF + chunk * PART, cond)
        cond_shift(chunk).start()
    for chunk in range(CHUNKS):
        load(0, HALF + chunk * PART).wait()
        pack(raw, 0, HALF + chunk * PART, val)
        load(1, chunk * PART).wait()
        pack(raw, 1, chunk * PART, cond)
    for copy in constants:
        copy.wait()

    def pair_weight(position):
        gap = jnp.full((8, 128), cond_energy[0] - val_energy[position], jnp.float32)
        return (jnp.sqrt(4.0 / gap) * (1.0 / GRID**1.5))[0:1, 0:1]

    def add_part(val_ref, val_at, cond_ref, cond_at, first, which, size=PART):
        accumulate(
            val_ref[pl.ds(val_at, size)], cond_ref[pl.ds(cond_at, size)], first,
            width, depth, height, total.at[which]
        )

    high, low = col // 8, col % 8
    near = (high * 8, (1 - high) * 8)
    x_at, y_at, core = row // 4, row % 4 // 2, row % 2

    def line(which, offset):
        return near[which] + (low + offset + 8) % 8

    def ring(which, offset, own_core=True):
        y_of = y_at if which == 0 else 1 - y_at
        core_of = core if own_core else 1 - core
        return (x_at + offset + 4) % 4 * 4 + y_of * 2 + core_of

    up, down, across = (row, line(0, 1)), (row, line(0, -1)), (row, line(1, 0))
    right, left = (ring(0, 1), col), (ring(0, -1), col)
    beside, mate = (ring(1, 0), col), (ring(0, 0, False), col)
    sent = []

    def deal(turn):
        @pl.loop(0, 16 // GROUP)
        def _(step):
            first = (row // GROUP + step) % (16 // GROUP) * GROUP
            select_group(first, table, cells, lanes, signs, pieces.at[turn])
            for near_block in range(GROUP):
                block = first + near_block

                @pl.when(block != row)
                def _():
                    remote(
                        pieces.at[turn, block], row_in.at[turn, row],
                        deal_send.at[turn, 0], deal_recv.at[turn, 0], (block, col)
                    ).start()

                @pl.when(block != col)
                def _():
                    remote(
                        pieces.at[turn, block], col_in.at[turn, col],
                        deal_send.at[turn, 1], deal_recv.at[turn, 1], (row, block)
                    ).start()

        row_in[turn, pl.ds(row, 1)] = pieces[turn, pl.ds(row, 1)]
        col_in[turn, pl.ds(col, 1)] = pieces[turn, pl.ds(col, 1)]

    def dealt(turn, which):
        landing = (row_in, col_in)[which]
        return remote(
            pieces.at[turn, pl.ds(0, 15)], landing.at[turn, pl.ds(0, 15)],
            deal_send.at[turn, which], deal_recv.at[turn, which], (row, col)
        )

    def ring_tools(turn, which):
        full = (row_full, col_full)[which].at[turn]
        sends = (row_send, col_send)[which].at[turn]
        recvs = (row_recv, col_recv)[which].at[turn]
        used = []

        def push(slot, *devices):
            for device in devices:
                copy = remote(
                    full.at[slot], full.at[slot], sends.at[len(used)], recvs.at[slot], device
                )
                copy.start()
                used.append(copy)
                sent.append(copy)

        def got(slot):
            remote(
                full.at[slot], full.at[slot], sends.at[0], recvs.at[slot], (row, col)
            ).wait_recv()

        def step(slot, *devices):
            got(slot)
            push(slot, *devices)

        return push, got, step

    def row_spread(turn):
        push, got, step = ring_tools(turn, 0)
        dealt(turn, 0).wait_recv()
        arrange(row_in.at[turn], wide, row_full.at[turn], col)
        push(col, up, down, across, (row, line(1, 1)), (row, line(1, -1)))
        yield
        step(line(0, -1), up)
        step(line(0, 1), down)
        got(line(1, 0))
        yield
        step(line(1, -1), up)
        step(line(1, 1), down)
        yield
        step(line(0, -2), up, (row, line(0, 2)))
        step(line(0, 2), down)
        yield
        step(line(1, 2), down, (row, line(0, -2)))
        step(line(1, -2), up)
        yield
        got(line(0, -3))
        got(line(0, 3))
        got(line(1, -3))
        got(line(1, 3))
        got(line(0, -4))
        got(line(1, 4))
        yield

    def col_spread(turn):
        push, got, step = ring_tools(turn, 1)
        dealt(turn, 1).wait_recv()
        arrange(col_in.at[turn], wide, col_full.at[turn], row)
        push(row, beside, right, left, mate)
        push(row, *[(ring(which, offset), col) for which, offset in ((1, 1), (1, -1), (0, 2), (1, 2))])
        yield
        for which, offset in ((1, 0), (0, 1), (0, -1)):
            step(ring(which, offset), mate)
        yield
        for which, offset in ((1, 1), (1, -1), (0, 2), (1, 2)):
            step(ring(which, offset), mate)
        yield
        for which in range(2):
            for offset in (0, -1, 1, 2):
                got(ring(which, offset, False))
        yield
        for kind in range(2):
            block = col_full[turn, :, kind * 16 : kind * 16 + 16, :].reshape(256, 1024)
            turned = jnp.dot(swap[...], block, preferred_element_type=jnp.float32)
            ordered[:, kind * 16 : kind * 16 + 16, :] = turned.astype(jnp.bfloat16).reshape(
                16, 16, 1024
            )
        yield

    def product(turn, slots, strip):
        window = pl.ds(pl.multiple_of(strip * 256, 256), 256)
        left = jnp.concatenate([row_full[turn, slot, :, window] for slot in slots], axis=0)
        right_side = jnp.concatenate([ordered[slot] for slot in slots], axis=0)
        return window, lax.dot_general(
            left, right_side, (((0,), (0,)), ((), ())), preferred_element_type=jnp.float32
        )

    def first_product():
        @pl.loop(0, 4)
        def _(strip):
            window, values = product(0, range(16), strip)
            gram[window, :] = values

    def gather_product(slots):
        @pl.loop(0, 4)
        def _(strip):
            window, values = product(1, slots, strip)
            gram[window, :] += values

    def last_product(slots):
        @pl.loop(0, 4)
        def _(strip):
            window, values = product(1, slots, strip)
            gram[window, :] = scale * (gram[window, :] + values)

    total[...] = jnp.zeros_like(total)

    @pl.loop(0, FOLD // WIDE_PART)
    def _(step):
        at = step * WIDE_PART
        add_part(val, at, cond, at, at, 0, WIDE_PART)

    merged(total.at[0], merge, cube)
    total[0] = jnp.zeros_like(total[0])
    fill_table(cube, pair_weight(here), table)
    deal(0)
    row_early, col_early = row_spread(0), col_spread(0)
    row_late, col_late = row_spread(1), col_spread(1)
    cube_copy = remote(cube_sent, cube_got, cube_sem.at[0], cube_sem.at[1], next_device)

    def cond_part(chunk):
        add_part(val, HALF + chunk * PART, got_cond, chunk * PART, HALF + chunk * PART, 0)

    def val_part(chunk):
        val_shift(chunk).wait_recv()
        add_part(got_val, chunk * PART, cond, chunk * PART, chunk * PART, 1)

    cond_shift(0).wait_recv()
    cond_part(0)
    val_part(0)
    cond_shift(1).wait_recv()
    cond_part(1)
    val_part(1)
    next(col_early)
    cond_shift(2).wait_recv()
    next(row_early)
    cond_part(2)
    merged(total.at[0], merge, cube_sent)
    cube_copy.start()
    val_part(2)
    merged(total.at[1], merge, cube)
    next(col_early)
    cube_copy.wait_recv()
    cube[...] += cube_got[...]
    fill_table(cube, pair_weight(before), table)
    next(row_early)
    next(row_early)
    deal(1)
    next(row_early)
    next(row_early)
    next(col_early)
    next(row_late)
    next(col_late)
    next(col_early)
    next(row_early)
    next(row_late)
    next(row_late)
    next(col_early)
    first_product()
    next(row_late)
    next(row_late)
    next(col_late)
    next(col_late)
    next(col_late)
    next(col_late)
    gather_product(
        [col, line(1, 0)]
        + [line(which, offset) for which in range(2) for offset in (1, -1, 2, -2)]
    )
    next(row_late)
    last_product(
        [line(0, 3), line(0, -3), line(0, -4), line(1, 3), line(1, -3), line(1, 4)]
    )
    for turn in range(2):
        for which in range(2):
            dealt(turn, which).wait_send()
    for chunk in range(CHUNKS):
        val_shift(chunk).wait_send()
        cond_shift(chunk).wait_send()
    cube_copy.wait_send()
    for copy in sent:
        copy.wait_send()

def response(valence, conduction, val_energy, cond_energy, sphere_index, scale):
    anywhere = pl.BlockSpec(memory_space=pl.ANY)
    scalars = pl.BlockSpec(memory_space=pltpu.SMEM)
    dma = pltpu.SemaphoreType.DMA
    f32, bf16 = jnp.float32, jnp.bfloat16
    view = (4, FOLD, GRID, GRID)
    return pl.pallas_call(
        functools.partial(panel_kernel, scale),
        out_shape=pltpu.VMEM((1024, 1024), jnp.float32),
        in_specs=[
            anywhere, anywhere, scalars, scalars, pl.BlockSpec(memory_space=pltpu.VMEM), scalars,
            anywhere, anywhere, anywhere, anywhere,
        ],
        out_specs=pl.BlockSpec(memory_space=pltpu.VMEM),
        scratch_shapes=[
            pltpu.VMEM((2, 4, FOLD, GRID, GRID), bf16),
            pltpu.VMEM((FOLD, 3, GRID, 128), bf16),
            pltpu.VMEM((FOLD, 3, GRID, 128), bf16),
            pltpu.VMEM((HALF, 3, GRID, 128), bf16),
            pltpu.VMEM((HALF, 3, GRID, 128), bf16),
            pltpu.VMEM((768, 256), bf16),
            pltpu.VMEM((128, 192), bf16),
            pltpu.VMEM((4, 64, 1024), bf16),
            pltpu.VMEM((256, 256), bf16),
            pltpu.VMEM((2, 4, 2, 2, 4, 32, 128), f32),
            pltpu.VMEM((64, 512), f32),
            pltpu.VMEM((64, 512), f32),
            pltpu.VMEM((64, 512), f32),
            pltpu.VMEM((128, 128), f32),
            pltpu.VMEM((128, 128), jnp.int32),
            pltpu.VMEM((128, 128), f32),
            pltpu.VMEM((128, 256), bf16),
            pltpu.VMEM((2, 16, 16, 128), bf16),
            pltpu.VMEM((2, 16, 16, 128), bf16),
            pltpu.VMEM((2, 16, 16, 128), bf16),
            pltpu.VMEM((256, 128), f32),
            pltpu.VMEM((2, 16, 32, 1024), bf16),
            pltpu.VMEM((2, 16, 32, 1024), bf16),
            pltpu.VMEM((16, 32, 1024), bf16),
            dma((4 * CHUNKS,)),
            dma((4,)),
            dma((2, CHUNKS)),
            dma((2, CHUNKS)),
            dma((2,)),
            dma((2, 2)),
            dma((2, 2)),
            dma((2, 15)),
            dma((2, 16)),
            dma((2, 15)),
            dma((2, 16)),
        ],
        compiler_params=pltpu.CompilerParams(
            collective_id=0, has_side_effects=True, vmem_limit_bytes=59 * 2**20
        ),
        name="response",
    )(
        valence.reshape(view), conduction.reshape(view), val_energy, cond_energy,
        sphere_index.reshape(128, 128), width_table(), depth_table(), height_table(), merge_table(),
        swap_table(),
    )


def finish_kernel(source, target, sem):
    strips = [pl.ds(strip * 256, 256) for strip in range(4)]
    copies = [
        pltpu.make_async_copy(source.at[strip], target.at[strip], sem.at[number])
        for number, strip in enumerate(strips)
    ]
    for copy in copies:
        copy.start()
    for copy in copies:
        copy.wait()


def finished(values):
    return pl.pallas_call(
        finish_kernel,
        out_shape=jax.ShapeDtypeStruct((1024, 1024), jnp.float32),
        in_specs=[pl.BlockSpec(memory_space=pltpu.VMEM)],
        out_specs=pl.BlockSpec(memory_space=pl.ANY),
        scratch_shapes=[pltpu.SemaphoreType.DMA((4,))],
        compiler_params=pltpu.CompilerParams(vmem_limit_bytes=2**20),
        name="finished",
    )(values)


def local(valence, conduction, val_energy, cond_energy, sphere_index):
    devices = lax.axis_size("row") * lax.axis_size("col")
    scale = -1.0 / math.sqrt(2 * devices)
    return finished(
        response(valence, conduction, val_energy, cond_energy, sphere_index, scale)
    )


def solution(mesh):
    placed = (
        P(("row", "col"), None, None, None),
        P(("row", "col"), None, None, None),
        P(),
        P(("row", "col")),
        P(),
    )
    return jax.shard_map(
        local, mesh=mesh, in_specs=placed, out_specs=P("row", "col"), check_vma=False
    )
```

```python
import functools
import math

import jax
import jax.numpy as jnp
import numpy as np
from jax import lax
from jax.experimental import pallas as pl
from jax.experimental.pallas import tpu as pltpu
from jax.sharding import PartitionSpec as P

GRID = 96
GMAX = 15
FOLD = 24
PART = 4
CHUNKS = 3
HALF = 12
WIDE_PART = 8
GROUP = 4
ROWS = 16
COLS = 16
MESH = pl.DeviceIdType.MESH


def split_table(values):
    high = np.asarray(values, np.float32).astype(jnp.bfloat16)
    low = (np.asarray(values, np.float64) - high.astype(np.float64)).astype(jnp.bfloat16)
    return high, low


def depth_table():
    angle = 2.0 * np.pi * (np.outer(np.arange(GRID), np.arange(16)) % GRID) / GRID
    rows = np.concatenate([np.cos(angle), -np.sin(angle)], axis=1)
    table = np.zeros((3, 128, 128))
    for third in range(3):
        table[third, :GRID, third * 32 : third * 32 + 32] = rows
        table[third, GRID:, 96:] = rows[third * 32 : third * 32 + 32]
    high, low = split_table(table.reshape(384, 128))
    wide = np.concatenate([high, low], axis=1)
    return np.concatenate([wide, wide], axis=0)


def height_table():
    freq = np.arange(32) - GMAX
    angle = 2.0 * np.pi * (np.outer(freq, np.arange(GRID)) % GRID) / GRID
    high, low = split_table(np.concatenate([np.cos(angle), np.sin(angle)], axis=0))
    return np.concatenate([np.concatenate([high, high], 1), np.concatenate([low, low], 1)], 0)


def width_table():
    angle = 2.0 * np.pi * (np.outer(np.arange(FOLD), np.arange(16)) % GRID) / GRID
    return np.concatenate([np.cos(angle), np.sin(angle)], axis=1).astype(np.float32)


def merge_table():
    table = np.zeros((4, 2, 2, 16, 2, 2, 4, 2, 16))
    for cls in range(4):
        for side in range(2):
            sign = 1 - 2 * side
            for cs in range(2):
                for cy in range(2):
                    for quarter in range(4):
                        for cz in range(2):
                            turns = -sign * cls * quarter - cy + cz
                            turns += -sign if cs else 0
                            value = (1, 1j, -1, -1j)[turns % 4]
                            for gz in range(16):
                                table[cls, 0, side, gz, cs, cy, quarter, cz, gz] = value.real if isinstance(value, complex) else value
                                table[cls, 1, side, gz, cs, cy, quarter, cz, gz] = value.imag if isinstance(value, complex) else 0
    table = table.reshape(4, 64, 512)
    return np.concatenate([table, table], axis=2).astype(jnp.bfloat16)


def swap_table():
    table = np.zeros((16, 16, 16, 16), np.float32)
    for first in range(16):
        for second in range(16):
            table[first, second, second, first] = 1.0
    return table.reshape(256, 256).astype(jnp.bfloat16)


def remote(source, target, send_sem, recv_sem, device):
    return pltpu.make_async_remote_copy(
        src_ref=source,
        dst_ref=target,
        send_sem=send_sem,
        recv_sem=recv_sem,
        device_id=device,
        device_id_type=MESH,
    )


def two_parts(values):
    high = values.astype(jnp.bfloat16)
    return high, (values - high.astype(jnp.float32)).astype(jnp.bfloat16)


def pack(raw, which, start, out):
    extra = raw[which, 3, start : start + PART].astype(jnp.float32)
    for third in range(3):
        main = raw[which, third, start : start + PART].astype(jnp.float32)
        piece = extra[:, :, third * 32 : third * 32 + 32]
        out[start : start + PART, third] = jnp.concatenate([main, piece], axis=2).astype(
            jnp.bfloat16
        )


def accumulate(val, cond, here, width, depth, height, total):
    size = val.shape[0]
    density = val.astype(jnp.float32) * cond.astype(jnp.float32)
    columns = [
        part[:, third].reshape(size * GRID, 128)
        for part in two_parts(density)
        for third in range(3)
    ]
    deep = jnp.dot(
        jnp.concatenate(columns, axis=1), depth[...], preferred_element_type=jnp.float32
    )
    high, low = two_parts(deep[:, :128] + deep[:, 128:])
    sides = [
        jnp.concatenate([high[s : s + GRID], low[s : s + GRID]], axis=0)
        for s in range(0, size * GRID, GRID)
    ]
    tall = jnp.dot(
        height[...], jnp.concatenate(sides, axis=1), preferred_element_type=jnp.float32
    )
    tall = tall[:64] + tall[64:]
    for cy in range(2):
        parts = [
            tall[cy * 32 : cy * 32 + 32, 128 * near : 128 * near + 128] for near in range(size)
        ]
        for cs in range(2):
            for freq in range(cs, 16):
                entry = cs * 16 + freq
                sums = total[freq % 4, cs, cy, freq // 4]
                for near in range(size):
                    sums += width[here + near, entry] * parts[near]
                total[freq % 4, cs, cy, freq // 4] = sums


def merged(total, merge, out):
    for cls in range(4):
        full = jnp.concatenate(
            [total[cls, cs, cy].reshape(128, 128) for cs in range(2) for cy in range(2)], axis=1
        )
        out[:, cls * 128 : cls * 128 + 128] = lax.dot_general(
            merge[cls],
            jnp.concatenate(two_parts(full), axis=1),
            (((1,), (1,)), ((), ())),
            preferred_element_type=jnp.float32,
        )


def sphere_codes(sphere, cells, lanes, signs):
    index = sphere[...]
    upper = ((index >> 5) * 43691) >> 17
    x_part = ((index >> 10) * 7282) >> 16

    def centred(values):
        return jnp.where(values > GRID // 2, values - GRID, values)

    gx = centred(x_part)
    gy = centred(upper - GRID * x_part)
    gz = centred(index - GRID * upper)
    sign = jnp.where(gz < 0, -1, 1)
    gx, gy, gz = gx * sign, gy * sign, gz * sign
    size = jnp.abs(gx)
    cell = (size & 3) * 128 + (size >> 2) * 32 + gy + GMAX
    cells[...] = (cell & 255).astype(jnp.float32)
    lanes[...] = (cell >> 8) * 32 + jnp.where(gx < 0, 16, 0) + gz
    signs[...] = sign.astype(jnp.float32)


def fill_table(cube, weight, table):
    for part in range(2):
        for half in range(2):
            start = part * 64 + half * 32
            block = cube[part * 32 : part * 32 + 32, half * 256 : half * 256 + 256]
            table[start : start + 32, :] = (block * weight).astype(jnp.bfloat16)


def select_group(first, table, cells, lanes, signs, out):
    start = pl.multiple_of(first * 8, 8)
    cell = cells[pl.ds(start, GROUP * 8), :].astype(jnp.bfloat16)
    lane = lanes[pl.ds(start, GROUP * 8), :]
    sign = signs[pl.ds(start, GROUP * 8), :]
    count = lax.broadcasted_iota(jnp.int32, (256, 128), 0).astype(jnp.float32).astype(jnp.bfloat16)
    one, zero = jnp.bfloat16(1), jnp.bfloat16(0)
    hot = [jnp.where(count == cell[c : c + 1, :], one, zero) for c in range(GROUP * 8)]
    found = jnp.dot(
        table[...], jnp.concatenate(hot, axis=1), preferred_element_type=jnp.float32
    )
    deep = lax.broadcasted_iota(jnp.int32, (64, 128), 0)
    groups = lax.broadcasted_iota(jnp.int32, (16, 128), 1) >> 3
    adder = (groups == lax.broadcasted_iota(jnp.int32, (16, 128), 0)).astype(jnp.bfloat16)
    for block in range(GROUP):
        parts = []
        for c in range(block * 8, block * 8 + 8):
            keep = deep == lane[c : c + 1, :]
            for part in range(2):
                mask = jnp.where(keep, sign[c : c + 1, :] if part else 1.0, 0.0)
                values = found[part * 64 : part * 64 + 64, c * 128 : c * 128 + 128] * mask
                parts.append(jnp.sum(values.reshape(8, 8, 128), axis=0))
        stacked = jnp.concatenate(parts, axis=0).astype(jnp.bfloat16)
        out[first + block] = jnp.dot(
            adder, stacked, preferred_element_type=jnp.float32
        ).astype(jnp.bfloat16)


def arrange(landing, wide, full, slot):
    wide[...] = landing[...].astype(jnp.float32).reshape(256, 128)
    for chunk in range(8):
        for kind in range(2):
            lines = wide[pl.ds(chunk * 2 + kind, 16, stride=16), :]
            full[slot, kind * 16 : kind * 16 + 16, chunk * 128 : chunk * 128 + 128] = (
                lines.astype(jnp.bfloat16)
            )


def panel_kernel(
    scale, val_hbm, cond_hbm, val_energy, cond_energy, sphere, width, depth_hbm, height_hbm, merge_hbm,
    swap_hbm, gram,
    raw, val, cond, got_val, got_cond, depth, height, merge, swap, total, cube, cube_sent, cube_got,
    cells, lanes, signs, table, pieces, row_in, col_in, wide, row_full, col_full,
    ordered, load_sem, table_sem, shift_send, shift_recv, cube_sem, deal_send, deal_recv,
    row_send, row_recv, col_send, col_recv
):
    row = lax.axis_index("row")
    col = lax.axis_index("col")
    here = row * COLS + col
    after = (here + 1) % (ROWS * COLS)
    before = (here + ROWS * COLS - 1) % (ROWS * COLS)
    next_device = (after // COLS, after % COLS)
    last_device = (before // COLS, before % COLS)

    loads = {}
    for chunk in range(CHUNKS):
        for which, source, start in (
            (0, val_hbm, chunk * PART), (1, cond_hbm, HALF + chunk * PART),
        ):
            loads[which, start] = (source, len(loads))
    for chunk in range(CHUNKS):
        for which, source, start in (
            (0, val_hbm, HALF + chunk * PART), (1, cond_hbm, chunk * PART),
        ):
            loads[which, start] = (source, len(loads))

    def load(which, start):
        source, number = loads[which, start]
        window = pl.ds(start, PART)
        return pltpu.make_async_copy(
            source.at[:, window], raw.at[which, :, window], load_sem.at[number]
        )

    for which, start in loads:
        load(which, start).start()
    constants = [
        pltpu.make_async_copy(source, target, table_sem.at[number])
        for number, (source, target) in enumerate(
            ((depth_hbm, depth), (height_hbm, height), (merge_hbm, merge), (swap_hbm, swap))
        )
    ]
    for copy in constants:
        copy.start()

    barrier = pltpu.get_barrier_semaphore()
    for step in range(1, 16):
        for device in (((row + step) % ROWS, col), (row, (col + step) % COLS)):
            pl.semaphore_signal(barrier, inc=1, device_id=device, device_id_type=MESH)
    for device in (next_device, last_device):
        pl.semaphore_signal(barrier, inc=1, device_id=device, device_id_type=MESH)
    sphere_codes(sphere, cells, lanes, signs)
    pl.semaphore_wait(barrier, 32)

    def val_shift(chunk):
        window = pl.ds(chunk * PART, PART)
        return remote(
            val.at[window], got_val.at[window],
            shift_send.at[0, chunk], shift_recv.at[0, chunk], next_device
        )

    def cond_shift(chunk):
        return remote(
            cond.at[pl.ds(HALF + chunk * PART, PART)], got_cond.at[pl.ds(chunk * PART, PART)],
            shift_send.at[1, chunk], shift_recv.at[1, chunk], last_device
        )

    for chunk in range(CHUNKS):
        load(0, chunk * PART).wait()
        pack(raw, 0, chunk * PART, val)
        val_shift(chunk).start()
        load(1, HALF + chunk * PART).wait()
        pack(raw, 1, HALF + chunk * PART, cond)
        cond_shift(chunk).start()
    for chunk in range(CHUNKS):
        load(0, HALF + chunk * PART).wait()
        pack(raw, 0, HALF + chunk * PART, val)
        load(1, chunk * PART).wait()
        pack(raw, 1, chunk * PART, cond)
    for copy in constants:
        copy.wait()

    def pair_weight(position):
        gap = jnp.full((8, 128), cond_energy[0] - val_energy[position], jnp.float32)
        return (jnp.sqrt(4.0 / gap) * (1.0 / GRID**1.5))[0:1, 0:1]

    def add_part(val_ref, val_at, cond_ref, cond_at, first, which, size=PART):
        accumulate(
            val_ref[pl.ds(val_at, size)], cond_ref[pl.ds(cond_at, size)], first,
            width, depth, height, total.at[which]
        )

    high, low = col // 8, col % 8
    near = (high * 8, (1 - high) * 8)
    x_at, y_at, core = row // 4, row % 4 // 2, row % 2

    def line(which, offset):
        return near[which] + (low + offset + 8) % 8

    def ring(which, offset, own_core=True):
        y_of = y_at if which == 0 else 1 - y_at
        core_of = core if own_core else 1 - core
        return (x_at + offset + 4) % 4 * 4 + y_of * 2 + core_of

    up, down, across = (row, line(0, 1)), (row, line(0, -1)), (row, line(1, 0))
    right, left = (ring(0, 1), col), (ring(0, -1), col)
    beside, mate = (ring(1, 0), col), (ring(0, 0, False), col)
    sent = []

    def deal(turn):
        @pl.loop(0, 16 // GROUP)
        def _(step):
            first = (row // GROUP + step) % (16 // GROUP) * GROUP
            select_group(first, table, cells, lanes, signs, pieces.at[turn])
            for near_block in range(GROUP):
                block = first + near_block

                @pl.when(block != row)
                def _():
                    remote(
                        pieces.at[turn, block], row_in.at[turn, row],
                        deal_send.at[turn, 0], deal_recv.at[turn, 0], (block, col)
                    ).start()

        @pl.loop(1, 16)
        def _(step):
            block = (col + step) % COLS
            remote(
                pieces.at[turn, block], col_in.at[turn, col],
                deal_send.at[turn, 1], deal_recv.at[turn, 1], (row, block)
            ).start()

        row_in[turn, pl.ds(row, 1)] = pieces[turn, pl.ds(row, 1)]
        col_in[turn, pl.ds(col, 1)] = pieces[turn, pl.ds(col, 1)]

    def dealt(turn, which):
        landing = (row_in, col_in)[which]
        return remote(
            pieces.at[turn, pl.ds(0, 15)], landing.at[turn, pl.ds(0, 15)],
            deal_send.at[turn, which], deal_recv.at[turn, which], (row, col)
        )

    def ring_tools(turn, which):
        full = (row_full, col_full)[which].at[turn]
        sends = (row_send, col_send)[which].at[turn]
        recvs = (row_recv, col_recv)[which].at[turn]
        used = []

        def push(slot, *devices):
            for device in devices:
                copy = remote(
                    full.at[slot], full.at[slot], sends.at[len(used)], recvs.at[slot], device
                )
                copy.start()
                used.append(copy)
                sent.append(copy)

        def got(slot):
            remote(
                full.at[slot], full.at[slot], sends.at[0], recvs.at[slot], (row, col)
            ).wait_recv()

        def step(slot, *devices):
            got(slot)
            push(slot, *devices)

        return push, got, step

    def row_spread(turn):
        push, got, step = ring_tools(turn, 0)
        dealt(turn, 0).wait_recv()
        arrange(row_in.at[turn], wide, row_full.at[turn], col)
        yield
        push(col, up, down, (row, line(1, 1)), (row, line(1, -1)), across)
        yield
        step(line(0, -1), up)
        step(line(0, 1), down)
        got(line(1, 0))
        yield
        step(line(1, -1), up)
        step(line(1, 1), down)
        yield
        step(line(0, -2), up, (row, line(0, 2)))
        step(line(0, 2), down)
        yield
        step(line(1, 2), down, (row, line(0, -2)))
        step(line(1, -2), up)
        yield
        got(line(0, -3))
        got(line(0, 3))
        got(line(1, -3))
        got(line(1, 3))
        got(line(0, -4))
        got(line(1, 4))
        yield

    def col_spread(turn):
        push, got, step = ring_tools(turn, 1)
        dealt(turn, 1).wait_recv()
        arrange(col_in.at[turn], wide, col_full.at[turn], row)
        yield
        opposite = (ring(0, 2), col)
        if turn == 0:
            push(row, right, left, opposite, beside, mate)
            yield
            step(ring(1, 0), right, left, opposite, mate)
            for offset in (1, -1, 2):
                step(ring(0, offset), mate)
            yield
            for offset in (1, -1, 2):
                step(ring(1, offset), mate)
            yield
        else:
            push(row, beside, right, left, mate, opposite)
            push(row, *[(ring(1, offset), col) for offset in (1, -1, 2)])
            yield
            for which, offset in ((1, 0), (0, 1), (0, -1)):
                step(ring(which, offset), mate)
            yield
            for which, offset in ((1, 1), (1, -1), (0, 2), (1, 2)):
                step(ring(which, offset), mate)
            yield
        for which in range(2):
            for offset in (0, -1, 1, 2):
                got(ring(which, offset, False))
        yield
        for kind in range(2):
            block = col_full[turn, :, kind * 16 : kind * 16 + 16, :].reshape(256, 1024)
            turned = jnp.dot(swap[...], block, preferred_element_type=jnp.float32)
            ordered[:, kind * 16 : kind * 16 + 16, :] = turned.astype(jnp.bfloat16).reshape(
                16, 16, 1024
            )
        yield

    def product(turn, slots, strip):
        window = pl.ds(pl.multiple_of(strip * 256, 256), 256)
        left = jnp.concatenate([row_full[turn, slot, :, window] for slot in slots], axis=0)
        right_side = jnp.concatenate([ordered[slot] for slot in slots], axis=0)
        return window, lax.dot_general(
            left, right_side, (((0,), (0,)), ((), ())), preferred_element_type=jnp.float32
        )

    def first_product():
        @pl.loop(0, 4)
        def _(strip):
            window, values = product(0, range(16), strip)
            gram[window, :] = values

    def gather_product(slots):
        @pl.loop(0, 4)
        def _(strip):
            window, values = product(1, slots, strip)
            gram[window, :] += values

    def last_product(slots):
        @pl.loop(0, 4)
        def _(strip):
            window, values = product(1, slots, strip)
            gram[window, :] = scale * (gram[window, :] + values)

    total[...] = jnp.zeros_like(total)

    @pl.loop(0, FOLD // WIDE_PART)
    def _(step):
        at = step * WIDE_PART
        add_part(val, at, cond, at, at, 0, WIDE_PART)

    merged(total.at[0], merge, cube)
    total[0] = jnp.zeros_like(total[0])
    fill_table(cube, pair_weight(here), table)
    deal(0)
    row_early, col_early = row_spread(0), col_spread(0)
    row_late, col_late = row_spread(1), col_spread(1)
    cube_copy = remote(cube_sent, cube_got, cube_sem.at[0], cube_sem.at[1], next_device)

    def cond_part(chunk):
        add_part(val, HALF + chunk * PART, got_cond, chunk * PART, HALF + chunk * PART, 0)

    def val_part(chunk):
        val_shift(chunk).wait_recv()
        add_part(got_val, chunk * PART, cond, chunk * PART, chunk * PART, 1)

    cond_shift(0).wait_recv()
    cond_part(0)
    val_part(0)
    cond_shift(1).wait_recv()
    cond_part(1)
    val_part(1)
    next(col_early)
    next(row_early)
    cond_shift(2).wait_recv()
    next(row_early)
    cond_part(2)
    merged(total.at[0], merge, cube)
    cube_sent[...] = cube[...].astype(jnp.bfloat16)
    cube_copy.start()
    next(col_early)
    val_part(2)
    merged(total.at[1], merge, cube)
    cube_copy.wait_recv()
    cube[...] += cube_got[...].astype(jnp.float32)
    fill_table(cube, pair_weight(before), table)
    next(row_early)
    next(row_early)
    deal(1)
    next(row_early)
    next(row_early)
    next(col_early)
    next(row_late)
    next(row_late)
    next(col_late)
    next(col_late)
    next(col_early)
    next(row_early)
    next(row_late)
    next(row_late)
    next(col_early)
    next(col_late)
    next(row_late)
    next(row_late)
    next(col_late)
    next(col_early)
    first_product()
    next(col_late)
    next(col_late)
    gather_product(
        [col, line(1, 0)]
        + [line(which, offset) for which in range(2) for offset in (1, -1, 2, -2)]
    )
    next(row_late)
    last_product(
        [line(0, 3), line(0, -3), line(0, -4), line(1, 3), line(1, -3), line(1, 4)]
    )
    for turn in range(2):
        for which in range(2):
            dealt(turn, which).wait_send()
    for chunk in range(CHUNKS):
        val_shift(chunk).wait_send()
        cond_shift(chunk).wait_send()
    cube_copy.wait_send()
    for copy in sent:
        copy.wait_send()

def response(valence, conduction, val_energy, cond_energy, sphere_index, scale):
    anywhere = pl.BlockSpec(memory_space=pl.ANY)
    scalars = pl.BlockSpec(memory_space=pltpu.SMEM)
    dma = pltpu.SemaphoreType.DMA
    f32, bf16 = jnp.float32, jnp.bfloat16
    view = (4, FOLD, GRID, GRID)
    return pl.pallas_call(
        functools.partial(panel_kernel, scale),
        out_shape=pltpu.VMEM((1024, 1024), jnp.float32),
        in_specs=[
            anywhere, anywhere, scalars, scalars, pl.BlockSpec(memory_space=pltpu.VMEM), scalars,
            anywhere, anywhere, anywhere, anywhere,
        ],
        out_specs=pl.BlockSpec(memory_space=pltpu.VMEM),
        scratch_shapes=[
            pltpu.VMEM((2, 4, FOLD, GRID, GRID), bf16),
            pltpu.VMEM((FOLD, 3, GRID, 128), bf16),
            pltpu.VMEM((FOLD, 3, GRID, 128), bf16),
            pltpu.VMEM((HALF, 3, GRID, 128), bf16),
            pltpu.VMEM((HALF, 3, GRID, 128), bf16),
            pltpu.VMEM((768, 256), bf16),
            pltpu.VMEM((128, 192), bf16),
            pltpu.VMEM((4, 64, 1024), bf16),
            pltpu.VMEM((256, 256), bf16),
            pltpu.VMEM((2, 4, 2, 2, 4, 32, 128), f32),
            pltpu.VMEM((64, 512), f32),
            pltpu.VMEM((64, 512), bf16),
            pltpu.VMEM((64, 512), bf16),
            pltpu.VMEM((128, 128), f32),
            pltpu.VMEM((128, 128), jnp.int32),
            pltpu.VMEM((128, 128), f32),
            pltpu.VMEM((128, 256), bf16),
            pltpu.VMEM((2, 16, 16, 128), bf16),
            pltpu.VMEM((2, 16, 16, 128), bf16),
            pltpu.VMEM((2, 16, 16, 128), bf16),
            pltpu.VMEM((256, 128), f32),
            pltpu.VMEM((2, 16, 32, 1024), bf16),
            pltpu.VMEM((2, 16, 32, 1024), bf16),
            pltpu.VMEM((16, 32, 1024), bf16),
            dma((4 * CHUNKS,)),
            dma((4,)),
            dma((2, CHUNKS)),
            dma((2, CHUNKS)),
            dma((2,)),
            dma((2, 2)),
            dma((2, 2)),
            dma((2, 15)),
            dma((2, 16)),
            dma((2, 15)),
            dma((2, 16)),
        ],
        compiler_params=pltpu.CompilerParams(
            collective_id=0, has_side_effects=True, vmem_limit_bytes=59 * 2**20
        ),
        name="response",
    )(
        valence.reshape(view), conduction.reshape(view), val_energy, cond_energy,
        sphere_index.reshape(128, 128), width_table(), depth_table(), height_table(), merge_table(),
        swap_table(),
    )


def finish_kernel(source, target, sem):
    strips = [pl.ds(strip * 256, 256) for strip in range(4)]
    copies = [
        pltpu.make_async_copy(source.at[strip], target.at[strip], sem.at[number])
        for number, strip in enumerate(strips)
    ]
    for copy in copies:
        copy.start()
    for copy in copies:
        copy.wait()


def finished(values):
    return pl.pallas_call(
        finish_kernel,
        out_shape=jax.ShapeDtypeStruct((1024, 1024), jnp.float32),
        in_specs=[pl.BlockSpec(memory_space=pltpu.VMEM)],
        out_specs=pl.BlockSpec(memory_space=pl.ANY),
        scratch_shapes=[pltpu.SemaphoreType.DMA((4,))],
        compiler_params=pltpu.CompilerParams(vmem_limit_bytes=2**20),
        name="finished",
    )(values)


def local(valence, conduction, val_energy, cond_energy, sphere_index):
    devices = lax.axis_size("row") * lax.axis_size("col")
    scale = -1.0 / math.sqrt(2 * devices)
    return finished(
        response(valence, conduction, val_energy, cond_energy, sphere_index, scale)
    )


def solution(mesh):
    placed = (
        P(("row", "col"), None, None, None),
        P(("row", "col"), None, None, None),
        P(),
        P(("row", "col")),
        P(),
    )
    return jax.shard_map(
        local, mesh=mesh, in_specs=placed, out_specs=P("row", "col"), check_vma=False
    )
```

```python
import functools
import math

import jax
import jax.numpy as jnp
import numpy as np
from jax import lax
from jax.experimental import pallas as pl
from jax.experimental.pallas import tpu as pltpu
from jax.sharding import PartitionSpec as P

GRID = 96
GMAX = 15
FOLD = 24
PART = 4
CHUNKS = 3
HALF = 12
WIDE_PART = 8
GROUP = 4
ROWS = 16
COLS = 16
MESH = pl.DeviceIdType.MESH


def split_table(values):
    high = np.asarray(values, np.float32).astype(jnp.bfloat16)
    low = (np.asarray(values, np.float64) - high.astype(np.float64)).astype(jnp.bfloat16)
    return high, low


def depth_table():
    angle = 2.0 * np.pi * (np.outer(np.arange(GRID), np.arange(16)) % GRID) / GRID
    rows = np.concatenate([np.cos(angle), -np.sin(angle)], axis=1)
    table = np.zeros((3, 128, 128))
    for third in range(3):
        table[third, :GRID, third * 32 : third * 32 + 32] = rows
        table[third, GRID:, 96:] = rows[third * 32 : third * 32 + 32]
    high, low = split_table(table.reshape(384, 128))
    wide = np.concatenate([high, low], axis=1)
    return np.concatenate([wide, wide], axis=0)


def height_table():
    freq = np.arange(32) - GMAX
    angle = 2.0 * np.pi * (np.outer(freq, np.arange(GRID)) % GRID) / GRID
    high, low = split_table(np.concatenate([np.cos(angle), np.sin(angle)], axis=0))
    return np.concatenate([np.concatenate([high, high], 1), np.concatenate([low, low], 1)], 0)


def width_table():
    angle = 2.0 * np.pi * (np.outer(np.arange(FOLD), np.arange(16)) % GRID) / GRID
    return np.concatenate([np.cos(angle), np.sin(angle)], axis=1).astype(np.float32)


def merge_table():
    table = np.zeros((4, 2, 2, 16, 2, 2, 4, 2, 16))
    for cls in range(4):
        for side in range(2):
            sign = 1 - 2 * side
            for cs in range(2):
                for cy in range(2):
                    for quarter in range(4):
                        for cz in range(2):
                            turns = -sign * cls * quarter - cy + cz
                            turns += -sign if cs else 0
                            value = (1, 1j, -1, -1j)[turns % 4]
                            for gz in range(16):
                                table[cls, 0, side, gz, cs, cy, quarter, cz, gz] = value.real if isinstance(value, complex) else value
                                table[cls, 1, side, gz, cs, cy, quarter, cz, gz] = value.imag if isinstance(value, complex) else 0
    table = table.reshape(4, 64, 512)
    return np.concatenate([table, table], axis=2).astype(jnp.bfloat16)


def swap_table():
    table = np.zeros((16, 16, 16, 16), np.float32)
    for first in range(16):
        for second in range(16):
            table[first, second, second, first] = 1.0
    return table.reshape(256, 256).astype(jnp.bfloat16)


def remote(source, target, send_sem, recv_sem, device):
    return pltpu.make_async_remote_copy(
        src_ref=source,
        dst_ref=target,
        send_sem=send_sem,
        recv_sem=recv_sem,
        device_id=device,
        device_id_type=MESH,
    )


def two_parts(values):
    high = values.astype(jnp.bfloat16)
    return high, (values - high.astype(jnp.float32)).astype(jnp.bfloat16)


def pack(raw, which, start, out):
    extra = raw[which, 3, start : start + PART].astype(jnp.float32)
    for third in range(3):
        main = raw[which, third, start : start + PART].astype(jnp.float32)
        piece = extra[:, :, third * 32 : third * 32 + 32]
        out[start : start + PART, third] = jnp.concatenate([main, piece], axis=2).astype(
            jnp.bfloat16
        )


def accumulate(val, cond, here, width, depth, height, total):
    size = val.shape[0]
    density = val.astype(jnp.float32) * cond.astype(jnp.float32)
    columns = [
        part[:, third].reshape(size * GRID, 128)
        for part in two_parts(density)
        for third in range(3)
    ]
    deep = jnp.dot(
        jnp.concatenate(columns, axis=1), depth[...], preferred_element_type=jnp.float32
    )
    high, low = two_parts(deep[:, :128] + deep[:, 128:])
    sides = [
        jnp.concatenate([high[s : s + GRID], low[s : s + GRID]], axis=0)
        for s in range(0, size * GRID, GRID)
    ]
    tall = jnp.dot(
        height[...], jnp.concatenate(sides, axis=1), preferred_element_type=jnp.float32
    )
    tall = tall[:64] + tall[64:]
    for cy in range(2):
        parts = [
            tall[cy * 32 : cy * 32 + 32, 128 * near : 128 * near + 128] for near in range(size)
        ]
        for cs in range(2):
            for freq in range(cs, 16):
                entry = cs * 16 + freq
                sums = total[freq % 4, cs, cy, freq // 4]
                for near in range(size):
                    sums += width[here + near, entry] * parts[near]
                total[freq % 4, cs, cy, freq // 4] = sums


def merged(total, merge, out):
    for cls in range(4):
        full = jnp.concatenate(
            [total[cls, cs, cy].reshape(128, 128) for cs in range(2) for cy in range(2)], axis=1
        )
        out[:, cls * 128 : cls * 128 + 128] = lax.dot_general(
            merge[cls],
            jnp.concatenate(two_parts(full), axis=1),
            (((1,), (1,)), ((), ())),
            preferred_element_type=jnp.float32,
        )


def sphere_codes(sphere, cells, lanes, signs):
    index = sphere[...]
    upper = ((index >> 5) * 43691) >> 17
    x_part = ((index >> 10) * 7282) >> 16

    def centred(values):
        return jnp.where(values > GRID // 2, values - GRID, values)

    gx = centred(x_part)
    gy = centred(upper - GRID * x_part)
    gz = centred(index - GRID * upper)
    sign = jnp.where(gz < 0, -1, 1)
    gx, gy, gz = gx * sign, gy * sign, gz * sign
    size = jnp.abs(gx)
    cell = (size & 3) * 128 + (size >> 2) * 32 + gy + GMAX
    cells[...] = (cell & 255).astype(jnp.float32)
    lanes[...] = (cell >> 8) * 32 + jnp.where(gx < 0, 16, 0) + gz
    signs[...] = sign.astype(jnp.float32)


def fill_table(cube, weight, table):
    for part in range(2):
        for half in range(2):
            start = part * 64 + half * 32
            block = cube[part * 32 : part * 32 + 32, half * 256 : half * 256 + 256]
            table[start : start + 32, :] = (block * weight).astype(jnp.bfloat16)


def select_group(first, table, cells, lanes, signs, out):
    start = pl.multiple_of(first * 8, 8)
    cell = cells[pl.ds(start, GROUP * 8), :].astype(jnp.bfloat16)
    lane = lanes[pl.ds(start, GROUP * 8), :]
    sign = signs[pl.ds(start, GROUP * 8), :]
    count = lax.broadcasted_iota(jnp.int32, (256, 128), 0).astype(jnp.float32).astype(jnp.bfloat16)
    one, zero = jnp.bfloat16(1), jnp.bfloat16(0)
    hot = [jnp.where(count == cell[c : c + 1, :], one, zero) for c in range(GROUP * 8)]
    found = jnp.dot(
        table[...], jnp.concatenate(hot, axis=1), preferred_element_type=jnp.float32
    )
    deep = lax.broadcasted_iota(jnp.int32, (64, 128), 0)
    groups = lax.broadcasted_iota(jnp.int32, (16, 128), 1) >> 3
    adder = (groups == lax.broadcasted_iota(jnp.int32, (16, 128), 0)).astype(jnp.bfloat16)
    for block in range(GROUP):
        parts = []
        for c in range(block * 8, block * 8 + 8):
            keep = deep == lane[c : c + 1, :]
            for part in range(2):
                mask = jnp.where(keep, sign[c : c + 1, :] if part else 1.0, 0.0)
                values = found[part * 64 : part * 64 + 64, c * 128 : c * 128 + 128] * mask
                parts.append(jnp.sum(values.reshape(8, 8, 128), axis=0))
        stacked = jnp.concatenate(parts, axis=0).astype(jnp.bfloat16)
        out[first + block] = jnp.dot(
            adder, stacked, preferred_element_type=jnp.float32
        ).astype(jnp.bfloat16)


def arrange(landing, wide, full, slot):
    wide[...] = landing[...].astype(jnp.float32).reshape(256, 128)
    for chunk in range(8):
        for kind in range(2):
            lines = wide[pl.ds(chunk * 2 + kind, 16, stride=16), :]
            full[slot, kind * 16 : kind * 16 + 16, chunk * 128 : chunk * 128 + 128] = (
                lines.astype(jnp.bfloat16)
            )


def panel_kernel(
    scale, val_hbm, cond_hbm, val_energy, cond_energy, sphere, width, depth_hbm, height_hbm, merge_hbm,
    swap_hbm, gram,
    raw, val, cond, got_val, got_cond, depth, height, merge, swap, total, cube, cube_sent, cube_got,
    cells, lanes, signs, table, pieces, row_in, col_in, wide, row_full, col_full,
    ordered, load_sem, table_sem, shift_send, shift_recv, cube_sem, deal_send, deal_recv,
    row_send, row_recv, col_send, col_recv
):
    row = lax.axis_index("row")
    col = lax.axis_index("col")
    here = row * COLS + col
    after = (here + 1) % (ROWS * COLS)
    before = (here + ROWS * COLS - 1) % (ROWS * COLS)
    next_device = (after // COLS, after % COLS)
    last_device = (before // COLS, before % COLS)

    loads = {}
    for chunk in range(CHUNKS):
        for which, source, start in (
            (0, val_hbm, chunk * PART), (1, cond_hbm, HALF + chunk * PART),
        ):
            loads[which, start] = (source, len(loads))
    for chunk in range(CHUNKS):
        for which, source, start in (
            (0, val_hbm, HALF + chunk * PART), (1, cond_hbm, chunk * PART),
        ):
            loads[which, start] = (source, len(loads))

    def load(which, start):
        source, number = loads[which, start]
        window = pl.ds(start, PART)
        return pltpu.make_async_copy(
            source.at[:, window], raw.at[which, :, window], load_sem.at[number]
        )

    for which, start in loads:
        load(which, start).start()
    constants = [
        pltpu.make_async_copy(source, target, table_sem.at[number])
        for number, (source, target) in enumerate(
            ((depth_hbm, depth), (height_hbm, height), (merge_hbm, merge), (swap_hbm, swap))
        )
    ]
    for copy in constants:
        copy.start()

    barrier = pltpu.get_barrier_semaphore()
    for step in range(1, 16):
        for device in (((row + step) % ROWS, col), (row, (col + step) % COLS)):
            pl.semaphore_signal(barrier, inc=1, device_id=device, device_id_type=MESH)
    for device in (next_device, last_device):
        pl.semaphore_signal(barrier, inc=1, device_id=device, device_id_type=MESH)
    sphere_codes(sphere, cells, lanes, signs)
    pl.semaphore_wait(barrier, 32)

    def val_shift(chunk):
        window = pl.ds(chunk * PART, PART)
        return remote(
            val.at[window], got_val.at[window],
            shift_send.at[0, chunk], shift_recv.at[0, chunk], next_device
        )

    def cond_shift(chunk):
        return remote(
            cond.at[pl.ds(HALF + chunk * PART, PART)], got_cond.at[pl.ds(chunk * PART, PART)],
            shift_send.at[1, chunk], shift_recv.at[1, chunk], last_device
        )

    def send_part(chunk):
        val_shift(chunk).start()
        cond_shift(chunk).start()

    for chunk in range(CHUNKS):
        load(0, chunk * PART).wait()
        pack(raw, 0, chunk * PART, val)
        load(1, HALF + chunk * PART).wait()
        pack(raw, 1, HALF + chunk * PART, cond)
        send_part(chunk)
    for chunk in range(CHUNKS):
        load(0, HALF + chunk * PART).wait()
        pack(raw, 0, HALF + chunk * PART, val)
        load(1, chunk * PART).wait()
        pack(raw, 1, chunk * PART, cond)
    for copy in constants:
        copy.wait()

    def pair_weight(position):
        gap = jnp.full((8, 128), cond_energy[0] - val_energy[position], jnp.float32)
        return (jnp.sqrt(4.0 / gap) * (1.0 / GRID**1.5))[0:1, 0:1]

    def add_part(val_ref, val_at, cond_ref, cond_at, first, which, size=PART):
        accumulate(
            val_ref[pl.ds(val_at, size)], cond_ref[pl.ds(cond_at, size)], first,
            width, depth, height, total.at[which]
        )

    high, low = col // 8, col % 8
    near = (high * 8, (1 - high) * 8)
    x_at, y_at, core = row // 4, row % 4 // 2, row % 2

    def line(which, offset):
        return near[which] + (low + offset + 8) % 8

    def ring(which, offset, own_core=True):
        y_of = y_at if which == 0 else 1 - y_at
        core_of = core if own_core else 1 - core
        return (x_at + offset + 4) % 4 * 4 + y_of * 2 + core_of

    up, down, across = (row, line(0, 1)), (row, line(0, -1)), (row, line(1, 0))
    right, left = (ring(0, 1), col), (ring(0, -1), col)
    beside, mate = (ring(1, 0), col), (ring(0, 0, False), col)
    sent = []

    def deal(turn):
        @pl.loop(0, 16 // GROUP)
        def _(step):
            first = (row // GROUP + step) % (16 // GROUP) * GROUP
            select_group(first, table, cells, lanes, signs, pieces.at[turn])
            for near_block in range(GROUP):
                block = first + near_block

                @pl.when(block != row)
                def _():
                    remote(
                        pieces.at[turn, block], row_in.at[turn, row],
                        deal_send.at[turn, 0], deal_recv.at[turn, 0], (block, col)
                    ).start()

        @pl.loop(1, 16)
        def _(step):
            block = (col + step) % COLS
            remote(
                pieces.at[turn, block], col_in.at[turn, col],
                deal_send.at[turn, 1], deal_recv.at[turn, 1], (row, block)
            ).start()

        row_in[turn, pl.ds(row, 1)] = pieces[turn, pl.ds(row, 1)]
        col_in[turn, pl.ds(col, 1)] = pieces[turn, pl.ds(col, 1)]

    def dealt(turn, which):
        landing = (row_in, col_in)[which]
        return remote(
            pieces.at[turn, pl.ds(0, 15)], landing.at[turn, pl.ds(0, 15)],
            deal_send.at[turn, which], deal_recv.at[turn, which], (row, col)
        )

    def ring_tools(turn, which):
        full = (row_full, col_full)[which].at[turn]
        sends = (row_send, col_send)[which].at[turn]
        recvs = (row_recv, col_recv)[which].at[turn]
        used = []

        def push(slot, *devices):
            for device in devices:
                copy = remote(
                    full.at[slot], full.at[slot], sends.at[len(used)], recvs.at[slot], device
                )
                copy.start()
                used.append(copy)
                sent.append(copy)

        def got(slot):
            remote(
                full.at[slot], full.at[slot], sends.at[0], recvs.at[slot], (row, col)
            ).wait_recv()

        def step(slot, *devices):
            got(slot)
            push(slot, *devices)

        return push, got, step

    def row_spread(turn):
        push, got, step = ring_tools(turn, 0)
        dealt(turn, 0).wait_recv()
        arrange(row_in.at[turn], wide, row_full.at[turn], col)
        yield
        if turn == 0:
            push(col, up, down, across)
            yield
            step(line(0, -1), up, across)
            step(line(0, 1), down, across)
            yield
            step(line(0, 2), down, (row, line(0, -2)), across)
            step(line(0, -2), up, across)
            yield
            for offset in (3, -3, 4):
                step(line(0, offset), across)
            yield
            for offset in (0, 1, -1, 2, -2, 3, -3, 4):
                got(line(1, offset))
            yield
            return
        push(col, up, down, (row, line(1, 1)), (row, line(1, -1)), across)
        yield
        step(line(0, -1), up)
        step(line(0, 1), down)
        got(line(1, 0))
        yield
        step(line(1, -1), up)
        step(line(1, 1), down)
        yield
        step(line(0, -2), up, (row, line(0, 2)))
        step(line(0, 2), down)
        yield
        step(line(1, 2), down, (row, line(0, -2)))
        step(line(1, -2), up)
        yield
        got(line(0, -3))
        got(line(0, 3))
        got(line(1, -3))
        got(line(1, 3))
        got(line(0, -4))
        got(line(1, 4))
        yield

    def col_spread(turn):
        push, got, step = ring_tools(turn, 1)
        dealt(turn, 1).wait_recv()
        arrange(col_in.at[turn], wide, col_full.at[turn], row)
        yield
        opposite = (ring(0, 2), col)
        push(row, beside, right, left, opposite, mate)
        yield
        step(ring(1, 0), right, left, opposite, mate)
        for offset in (1, -1, 2):
            step(ring(0, offset), mate)
        yield
        for offset in (1, -1, 2):
            step(ring(1, offset), mate)
        yield
        for which in range(2):
            for offset in (0, -1, 1, 2):
                got(ring(which, offset, False))
        yield
        for kind in range(2):
            block = col_full[turn, :, kind * 16 : kind * 16 + 16, :].reshape(256, 1024)
            turned = jnp.dot(swap[...], block, preferred_element_type=jnp.float32)
            ordered[:, kind * 16 : kind * 16 + 16, :] = turned.astype(jnp.bfloat16).reshape(
                16, 16, 1024
            )
        yield

    def product(turn, slots, strip):
        window = pl.ds(pl.multiple_of(strip * 256, 256), 256)
        left = jnp.concatenate([row_full[turn, slot, :, window] for slot in slots], axis=0)
        right_side = jnp.concatenate([ordered[slot] for slot in slots], axis=0)
        return window, lax.dot_general(
            left, right_side, (((0,), (0,)), ((), ())), preferred_element_type=jnp.float32
        )

    def first_product(first, last):
        @pl.loop(first, last)
        def _(strip):
            window, values = product(0, range(16), strip)
            gram[window, :] = values

    def gather_product(slots):
        @pl.loop(0, 4)
        def _(strip):
            window, values = product(1, slots, strip)
            gram[window, :] += values

    def last_product(slots):
        @pl.loop(0, 4)
        def _(strip):
            window, values = product(1, slots, strip)
            gram[window, :] = scale * (gram[window, :] + values)

    total[...] = jnp.zeros_like(total)

    @pl.loop(0, FOLD // WIDE_PART)
    def _(step):
        at = step * WIDE_PART
        add_part(val, at, cond, at, at, 0, WIDE_PART)

    merged(total.at[0], merge, cube)
    total[0] = jnp.zeros_like(total[0])
    fill_table(cube, pair_weight(here), table)
    deal(0)
    row_early, col_early = row_spread(0), col_spread(0)
    row_late, col_late = row_spread(1), col_spread(1)
    cube_copy = remote(cube_sent, cube_got, cube_sem.at[0], cube_sem.at[1], next_device)

    def cond_part(chunk):
        add_part(val, HALF + chunk * PART, got_cond, chunk * PART, HALF + chunk * PART, 0)

    def val_part(chunk):
        val_shift(chunk).wait_recv()
        add_part(got_val, chunk * PART, cond, chunk * PART, chunk * PART, 1)

    cond_shift(0).wait_recv()
    cond_part(0)
    val_part(0)
    cond_shift(1).wait_recv()
    cond_part(1)
    val_part(1)
    next(col_early)
    next(row_early)
    cond_shift(2).wait_recv()
    next(row_early)
    cond_part(2)
    merged(total.at[0], merge, cube_sent)
    cube_copy.start()
    next(col_early)
    val_part(2)
    merged(total.at[1], merge, cube)
    cube_copy.wait_recv()
    cube[...] += cube_got[...]
    fill_table(cube, pair_weight(before), table)
    next(row_early)
    deal(1)
    next(row_early)
    next(col_early)
    next(row_late)
    next(row_late)
    next(col_late)
    next(col_late)
    next(col_early)
    next(row_early)
    next(row_late)
    next(col_late)
    next(row_late)
    next(col_early)
    next(col_early)
    next(row_late)
    next(row_late)
    next(col_late)
    next(row_early)
    first_product(0, 4)
    next(col_late)
    next(col_late)
    gather_product(
        [col, line(1, 0)]
        + [line(which, offset) for which in range(2) for offset in (1, -1, 2, -2)]
    )
    next(row_late)
    last_product(
        [line(0, 3), line(0, -3), line(0, -4), line(1, 3), line(1, -3), line(1, 4)]
    )
    for turn in range(2):
        for which in range(2):
            dealt(turn, which).wait_send()
    for chunk in range(CHUNKS):
        val_shift(chunk).wait_send()
        cond_shift(chunk).wait_send()
    cube_copy.wait_send()
    for copy in sent:
        copy.wait_send()

def response(valence, conduction, val_energy, cond_energy, sphere_index, scale):
    anywhere = pl.BlockSpec(memory_space=pl.ANY)
    scalars = pl.BlockSpec(memory_space=pltpu.SMEM)
    dma = pltpu.SemaphoreType.DMA
    f32, bf16 = jnp.float32, jnp.bfloat16
    view = (4, FOLD, GRID, GRID)
    return pl.pallas_call(
        functools.partial(panel_kernel, scale),
        out_shape=pltpu.VMEM((1024, 1024), jnp.float32),
        in_specs=[
            anywhere, anywhere, scalars, scalars, pl.BlockSpec(memory_space=pltpu.VMEM), scalars,
            anywhere, anywhere, anywhere, anywhere,
        ],
        out_specs=pl.BlockSpec(memory_space=pltpu.VMEM),
        scratch_shapes=[
            pltpu.VMEM((2, 4, FOLD, GRID, GRID), bf16),
            pltpu.VMEM((FOLD, 3, GRID, 128), bf16),
            pltpu.VMEM((FOLD, 3, GRID, 128), bf16),
            pltpu.VMEM((HALF, 3, GRID, 128), bf16),
            pltpu.VMEM((HALF, 3, GRID, 128), bf16),
            pltpu.VMEM((768, 256), bf16),
            pltpu.VMEM((128, 192), bf16),
            pltpu.VMEM((4, 64, 1024), bf16),
            pltpu.VMEM((256, 256), bf16),
            pltpu.VMEM((2, 4, 2, 2, 4, 32, 128), f32),
            pltpu.VMEM((64, 512), f32),
            pltpu.VMEM((64, 512), f32),
            pltpu.VMEM((64, 512), f32),
            pltpu.VMEM((128, 128), f32),
            pltpu.VMEM((128, 128), jnp.int32),
            pltpu.VMEM((128, 128), f32),
            pltpu.VMEM((128, 256), bf16),
            pltpu.VMEM((2, 16, 16, 128), bf16),
            pltpu.VMEM((2, 16, 16, 128), bf16),
            pltpu.VMEM((2, 16, 16, 128), bf16),
            pltpu.VMEM((256, 128), f32),
            pltpu.VMEM((2, 16, 32, 1024), bf16),
            pltpu.VMEM((2, 16, 32, 1024), bf16),
            pltpu.VMEM((16, 32, 1024), bf16),
            dma((4 * CHUNKS,)),
            dma((4,)),
            dma((2, CHUNKS)),
            dma((2, CHUNKS)),
            dma((2,)),
            dma((2, 2)),
            dma((2, 2)),
            dma((2, 15)),
            dma((2, 16)),
            dma((2, 15)),
            dma((2, 16)),
        ],
        compiler_params=pltpu.CompilerParams(
            collective_id=0, has_side_effects=True, vmem_limit_bytes=59 * 2**20
        ),
        name="response",
    )(
        valence.reshape(view), conduction.reshape(view), val_energy, cond_energy,
        sphere_index.reshape(128, 128), width_table(), depth_table(), height_table(), merge_table(),
        swap_table(),
    )


def finish_kernel(source, target, sem):
    strips = [pl.ds(strip * 256, 256) for strip in range(4)]
    copies = [
        pltpu.make_async_copy(source.at[strip], target.at[strip], sem.at[number])
        for number, strip in enumerate(strips)
    ]
    for copy in copies:
        copy.start()
    for copy in copies:
        copy.wait()


def finished(values):
    return pl.pallas_call(
        finish_kernel,
        out_shape=jax.ShapeDtypeStruct((1024, 1024), jnp.float32),
        in_specs=[pl.BlockSpec(memory_space=pltpu.VMEM)],
        out_specs=pl.BlockSpec(memory_space=pl.ANY),
        scratch_shapes=[pltpu.SemaphoreType.DMA((4,))],
        compiler_params=pltpu.CompilerParams(vmem_limit_bytes=2**20),
        name="finished",
    )(values)


def local(valence, conduction, val_energy, cond_energy, sphere_index):
    devices = lax.axis_size("row") * lax.axis_size("col")
    scale = -1.0 / math.sqrt(2 * devices)
    return finished(
        response(valence, conduction, val_energy, cond_energy, sphere_index, scale)
    )


def solution(mesh):
    placed = (
        P(("row", "col"), None, None, None),
        P(("row", "col"), None, None, None),
        P(),
        P(("row", "col")),
        P(),
    )
    return jax.shard_map(
        local, mesh=mesh, in_specs=placed, out_specs=P("row", "col"), check_vma=False
    )
```

```python
import functools
import math

import jax
import jax.numpy as jnp
import numpy as np
from jax import lax
from jax.experimental import pallas as pl
from jax.experimental.pallas import tpu as pltpu
from jax.sharding import PartitionSpec as P

GRID = 96
GMAX = 15
FOLD = 24
PART = 4
CHUNKS = 3
HALF = 12
WIDE_PART = 8
GROUP = 4
ROWS = 16
COLS = 16
MESH = pl.DeviceIdType.MESH


def split_table(values):
    high = np.asarray(values, np.float32).astype(jnp.bfloat16)
    low = (np.asarray(values, np.float64) - high.astype(np.float64)).astype(jnp.bfloat16)
    return high, low


def depth_table():
    angle = 2.0 * np.pi * (np.outer(np.arange(GRID), np.arange(16)) % GRID) / GRID
    rows = np.concatenate([np.cos(angle), -np.sin(angle)], axis=1)
    table = np.zeros((3, 128, 128))
    for third in range(3):
        table[third, :GRID, third * 32 : third * 32 + 32] = rows
        table[third, GRID:, 96:] = rows[third * 32 : third * 32 + 32]
    high, low = split_table(table.reshape(384, 128))
    wide = np.concatenate([high, low], axis=1)
    return np.concatenate([wide, wide], axis=0)


def height_table():
    freq = np.arange(32) - GMAX
    angle = 2.0 * np.pi * (np.outer(freq, np.arange(GRID)) % GRID) / GRID
    high, low = split_table(np.concatenate([np.cos(angle), np.sin(angle)], axis=0))
    return np.concatenate([np.concatenate([high, high], 1), np.concatenate([low, low], 1)], 0)


def width_table():
    angle = 2.0 * np.pi * (np.outer(np.arange(FOLD), np.arange(16)) % GRID) / GRID
    return np.concatenate([np.cos(angle), np.sin(angle)], axis=1).astype(np.float32)


def merge_table():
    table = np.zeros((4, 2, 2, 16, 2, 2, 4, 2, 16))
    for cls in range(4):
        for side in range(2):
            sign = 1 - 2 * side
            for cs in range(2):
                for cy in range(2):
                    for quarter in range(4):
                        for cz in range(2):
                            turns = -sign * cls * quarter - cy + cz
                            turns += -sign if cs else 0
                            value = (1, 1j, -1, -1j)[turns % 4]
                            for gz in range(16):
                                table[cls, 0, side, gz, cs, cy, quarter, cz, gz] = value.real if isinstance(value, complex) else value
                                table[cls, 1, side, gz, cs, cy, quarter, cz, gz] = value.imag if isinstance(value, complex) else 0
    table = table.reshape(4, 64, 512)
    return np.concatenate([table, table], axis=2).astype(jnp.bfloat16)


def swap_table():
    table = np.zeros((16, 16, 16, 16), np.float32)
    for first in range(16):
        for second in range(16):
            table[first, second, second, first] = 1.0
    return table.reshape(256, 256).astype(jnp.bfloat16)


def remote(source, target, send_sem, recv_sem, device):
    return pltpu.make_async_remote_copy(
        src_ref=source,
        dst_ref=target,
        send_sem=send_sem,
        recv_sem=recv_sem,
        device_id=device,
        device_id_type=MESH,
    )


def two_parts(values):
    high = values.astype(jnp.bfloat16)
    return high, (values - high.astype(jnp.float32)).astype(jnp.bfloat16)


def pack(raw, which, start, out):
    extra = raw[which, 3, start : start + PART].astype(jnp.float32)
    for third in range(3):
        main = raw[which, third, start : start + PART].astype(jnp.float32)
        piece = extra[:, :, third * 32 : third * 32 + 32]
        out[start : start + PART, third] = jnp.concatenate([main, piece], axis=2).astype(
            jnp.bfloat16
        )


def accumulate(val, cond, here, width, depth, height, total):
    size = val.shape[0]
    density = val.astype(jnp.float32) * cond.astype(jnp.float32)
    columns = [
        part[:, third].reshape(size * GRID, 128)
        for part in two_parts(density)
        for third in range(3)
    ]
    deep = jnp.dot(
        jnp.concatenate(columns, axis=1), depth[...], preferred_element_type=jnp.float32
    )
    high, low = two_parts(deep[:, :128] + deep[:, 128:])
    sides = [
        jnp.concatenate([high[s : s + GRID], low[s : s + GRID]], axis=0)
        for s in range(0, size * GRID, GRID)
    ]
    tall = jnp.dot(
        height[...], jnp.concatenate(sides, axis=1), preferred_element_type=jnp.float32
    )
    tall = tall[:64] + tall[64:]
    for cy in range(2):
        parts = [
            tall[cy * 32 : cy * 32 + 32, 128 * near : 128 * near + 128] for near in range(size)
        ]
        for cs in range(2):
            for freq in range(cs, 16):
                entry = cs * 16 + freq
                sums = total[freq % 4, cs, cy, freq // 4]
                for near in range(size):
                    sums += width[here + near, entry] * parts[near]
                total[freq % 4, cs, cy, freq // 4] = sums


def merged(total, merge, out):
    for cls in range(4):
        full = jnp.concatenate(
            [total[cls, cs, cy].reshape(128, 128) for cs in range(2) for cy in range(2)], axis=1
        )
        out[:, cls * 128 : cls * 128 + 128] = lax.dot_general(
            merge[cls],
            jnp.concatenate(two_parts(full), axis=1),
            (((1,), (1,)), ((), ())),
            preferred_element_type=jnp.float32,
        )


def sphere_codes(sphere, cells, lanes, signs):
    index = sphere[...]
    upper = ((index >> 5) * 43691) >> 17
    x_part = ((index >> 10) * 7282) >> 16

    def centred(values):
        return jnp.where(values > GRID // 2, values - GRID, values)

    gx = centred(x_part)
    gy = centred(upper - GRID * x_part)
    gz = centred(index - GRID * upper)
    sign = jnp.where(gz < 0, -1, 1)
    gx, gy, gz = gx * sign, gy * sign, gz * sign
    size = jnp.abs(gx)
    cell = (size & 3) * 128 + (size >> 2) * 32 + gy + GMAX
    cells[...] = (cell & 255).astype(jnp.float32)
    lanes[...] = (cell >> 8) * 32 + jnp.where(gx < 0, 16, 0) + gz
    signs[...] = sign.astype(jnp.float32)


def fill_table(cube, weight, table):
    for part in range(2):
        for half in range(2):
            start = part * 64 + half * 32
            block = cube[part * 32 : part * 32 + 32, half * 256 : half * 256 + 256]
            table[start : start + 32, :] = (block * weight).astype(jnp.bfloat16)


def select_group(first, table, cells, lanes, signs, out):
    start = pl.multiple_of(first * 8, 8)
    cell = cells[pl.ds(start, GROUP * 8), :].astype(jnp.bfloat16)
    lane = lanes[pl.ds(start, GROUP * 8), :]
    sign = signs[pl.ds(start, GROUP * 8), :]
    count = lax.broadcasted_iota(jnp.int32, (256, 128), 0).astype(jnp.float32).astype(jnp.bfloat16)
    one, zero = jnp.bfloat16(1), jnp.bfloat16(0)
    hot = [jnp.where(count == cell[c : c + 1, :], one, zero) for c in range(GROUP * 8)]
    found = jnp.dot(
        table[...], jnp.concatenate(hot, axis=1), preferred_element_type=jnp.float32
    )
    deep = lax.broadcasted_iota(jnp.int32, (64, 128), 0)
    groups = lax.broadcasted_iota(jnp.int32, (16, 128), 1) >> 3
    adder = (groups == lax.broadcasted_iota(jnp.int32, (16, 128), 0)).astype(jnp.bfloat16)
    for block in range(GROUP):
        parts = []
        for c in range(block * 8, block * 8 + 8):
            keep = deep == lane[c : c + 1, :]
            for part in range(2):
                mask = jnp.where(keep, sign[c : c + 1, :] if part else 1.0, 0.0)
                values = found[part * 64 : part * 64 + 64, c * 128 : c * 128 + 128] * mask
                parts.append(jnp.sum(values.reshape(8, 8, 128), axis=0))
        stacked = jnp.concatenate(parts, axis=0).astype(jnp.bfloat16)
        out[first + block] = jnp.dot(
            adder, stacked, preferred_element_type=jnp.float32
        ).astype(jnp.bfloat16)


def arrange(landing, wide, full, slot):
    wide[...] = landing[...].astype(jnp.float32).reshape(256, 128)
    for chunk in range(8):
        for kind in range(2):
            lines = wide[pl.ds(chunk * 2 + kind, 16, stride=16), :]
            full[slot, kind * 16 : kind * 16 + 16, chunk * 128 : chunk * 128 + 128] = (
                lines.astype(jnp.bfloat16)
            )


def panel_kernel(
    scale, val_hbm, cond_hbm, val_energy, cond_energy, sphere, width, depth_hbm, height_hbm, merge_hbm,
    swap_hbm, gram,
    raw, val, cond, got_val, got_cond, depth, height, merge, swap, total, cube, cube_sent, cube_got,
    cells, lanes, signs, table, pieces, row_in, col_in, wide, row_full, col_full,
    ordered, load_sem, table_sem, shift_send, shift_recv, cube_sem, deal_send, deal_recv,
    row_send, row_recv, col_send, col_recv
):
    row = lax.axis_index("row")
    col = lax.axis_index("col")
    here = row * COLS + col
    after = (here + 1) % (ROWS * COLS)
    before = (here + ROWS * COLS - 1) % (ROWS * COLS)
    next_device = (after // COLS, after % COLS)
    last_device = (before // COLS, before % COLS)

    loads = {}
    for chunk in range(CHUNKS):
        for which, source, start in (
            (0, val_hbm, chunk * PART), (1, cond_hbm, HALF + chunk * PART),
        ):
            loads[which, start] = (source, len(loads))
    for chunk in range(CHUNKS):
        for which, source, start in (
            (0, val_hbm, HALF + chunk * PART), (1, cond_hbm, chunk * PART),
        ):
            loads[which, start] = (source, len(loads))

    def load(which, start):
        source, number = loads[which, start]
        window = pl.ds(start, PART)
        return pltpu.make_async_copy(
            source.at[:, window], raw.at[which, :, window], load_sem.at[number]
        )

    for which, start in loads:
        load(which, start).start()
    constants = [
        pltpu.make_async_copy(source, target, table_sem.at[number])
        for number, (source, target) in enumerate(
            ((depth_hbm, depth), (height_hbm, height), (merge_hbm, merge), (swap_hbm, swap))
        )
    ]
    for copy in constants:
        copy.start()

    barrier = pltpu.get_barrier_semaphore()
    for step in range(1, 16):
        for device in (((row + step) % ROWS, col), (row, (col + step) % COLS)):
            pl.semaphore_signal(barrier, inc=1, device_id=device, device_id_type=MESH)
    for device in (next_device, last_device):
        pl.semaphore_signal(barrier, inc=1, device_id=device, device_id_type=MESH)
    sphere_codes(sphere, cells, lanes, signs)
    pl.semaphore_wait(barrier, 32)

    def val_shift(chunk):
        window = pl.ds(chunk * PART, PART)
        return remote(
            val.at[window], got_val.at[window],
            shift_send.at[0, chunk], shift_recv.at[0, chunk], next_device
        )

    def cond_shift(chunk):
        return remote(
            cond.at[pl.ds(HALF + chunk * PART, PART)], got_cond.at[pl.ds(chunk * PART, PART)],
            shift_send.at[1, chunk], shift_recv.at[1, chunk], last_device
        )

    def send_part(chunk):
        val_shift(chunk).start()
        cond_shift(chunk).start()

    for chunk in range(CHUNKS):
        load(0, chunk * PART).wait()
        pack(raw, 0, chunk * PART, val)
        load(1, HALF + chunk * PART).wait()
        pack(raw, 1, HALF + chunk * PART, cond)
        send_part(chunk)
    for chunk in range(CHUNKS):
        load(0, HALF + chunk * PART).wait()
        pack(raw, 0, HALF + chunk * PART, val)
        load(1, chunk * PART).wait()
        pack(raw, 1, chunk * PART, cond)
    for copy in constants:
        copy.wait()

    def pair_weight(position):
        gap = jnp.full((8, 128), cond_energy[0] - val_energy[position], jnp.float32)
        return (jnp.sqrt(4.0 / gap) * (1.0 / GRID**1.5))[0:1, 0:1]

    def add_part(val_ref, val_at, cond_ref, cond_at, first, which, size=PART):
        accumulate(
            val_ref[pl.ds(val_at, size)], cond_ref[pl.ds(cond_at, size)], first,
            width, depth, height, total.at[which]
        )

    high, low = col // 8, col % 8
    near = (high * 8, (1 - high) * 8)
    x_at, y_at, core = row // 4, row % 4 // 2, row % 2

    def line(which, offset):
        return near[which] + (low + offset + 8) % 8

    def ring(which, offset, own_core=True):
        y_of = y_at if which == 0 else 1 - y_at
        core_of = core if own_core else 1 - core
        return (x_at + offset + 4) % 4 * 4 + y_of * 2 + core_of

    up, down, across = (row, line(0, 1)), (row, line(0, -1)), (row, line(1, 0))
    right, left = (ring(0, 1), col), (ring(0, -1), col)
    beside, mate = (ring(1, 0), col), (ring(0, 0, False), col)
    sent = []

    def deal(turn):
        @pl.loop(0, 16 // GROUP)
        def _(step):
            first = (row // GROUP + step) % (16 // GROUP) * GROUP
            select_group(first, table, cells, lanes, signs, pieces.at[turn])
            for near_block in range(GROUP):
                block = first + near_block

                @pl.when(block != row)
                def _():
                    remote(
                        pieces.at[turn, block], row_in.at[turn, row],
                        deal_send.at[turn, 0], deal_recv.at[turn, 0], (block, col)
                    ).start()

        @pl.loop(1, 16)
        def _(step):
            block = (col + step) % COLS
            remote(
                pieces.at[turn, block], col_in.at[turn, col],
                deal_send.at[turn, 1], deal_recv.at[turn, 1], (row, block)
            ).start()

        row_in[turn, pl.ds(row, 1)] = pieces[turn, pl.ds(row, 1)]
        col_in[turn, pl.ds(col, 1)] = pieces[turn, pl.ds(col, 1)]

    def dealt(turn, which):
        landing = (row_in, col_in)[which]
        return remote(
            pieces.at[turn, pl.ds(0, 15)], landing.at[turn, pl.ds(0, 15)],
            deal_send.at[turn, which], deal_recv.at[turn, which], (row, col)
        )

    def ring_tools(turn, which):
        full = (row_full, col_full)[which].at[turn]
        sends = (row_send, col_send)[which].at[turn]
        recvs = (row_recv, col_recv)[which].at[turn]
        used = []

        def push(slot, *devices):
            for device in devices:
                copy = remote(
                    full.at[slot], full.at[slot], sends.at[len(used)], recvs.at[slot], device
                )
                copy.start()
                used.append(copy)
                sent.append(copy)

        def got(slot):
            remote(
                full.at[slot], full.at[slot], sends.at[0], recvs.at[slot], (row, col)
            ).wait_recv()

        def step(slot, *devices):
            got(slot)
            push(slot, *devices)

        return push, got, step

    def row_spread(turn):
        push, got, step = ring_tools(turn, 0)
        dealt(turn, 0).wait_recv()
        arrange(row_in.at[turn], wide, row_full.at[turn], col)
        yield
        if turn == 0:
            push(col, down, across)
            yield
            push(col, up)
            yield
            step(line(0, -1), up, across)
            step(line(0, 1), down, across)
            yield
            step(line(0, 2), down, (row, line(0, -2)), across)
            step(line(0, -2), up, across)
            yield
            for offset in (3, -3, 4):
                step(line(0, offset), across)
            yield
            for offset in (0, 1, -1, 2, -2, 3, -3, 4):
                got(line(1, offset))
            yield
            return
        push(col, up, down, (row, line(1, 1)), (row, line(1, -1)), across)
        yield
        step(line(0, -1), up)
        step(line(0, 1), down)
        got(line(1, 0))
        yield
        step(line(1, -1), up)
        step(line(1, 1), down)
        yield
        step(line(0, -2), up, (row, line(0, 2)))
        step(line(0, 2), down)
        yield
        step(line(1, 2), down, (row, line(0, -2)))
        step(line(1, -2), up)
        yield
        got(line(0, -3))
        got(line(0, 3))
        got(line(1, -3))
        got(line(1, 3))
        got(line(0, -4))
        got(line(1, 4))
        yield

    def col_spread(turn):
        push, got, step = ring_tools(turn, 1)
        dealt(turn, 1).wait_recv()
        arrange(col_in.at[turn], wide, col_full.at[turn], row)
        yield
        opposite = (ring(0, 2), col)
        push(row, beside, right, left, opposite, mate)
        yield
        step(ring(1, 0), right, left, opposite, mate)
        for offset in (1, -1, 2):
            step(ring(0, offset), mate)
        yield
        for offset in (1, -1, 2):
            step(ring(1, offset), mate)
        yield
        for which in range(2):
            for offset in (0, -1, 1, 2):
                got(ring(which, offset, False))
        yield
        for kind in range(2):
            block = col_full[turn, :, kind * 16 : kind * 16 + 16, :].reshape(256, 1024)
            turned = jnp.dot(swap[...], block, preferred_element_type=jnp.float32)
            ordered[:, kind * 16 : kind * 16 + 16, :] = turned.astype(jnp.bfloat16).reshape(
                16, 16, 1024
            )
        yield

    def product(turn, slots, strip):
        window = pl.ds(pl.multiple_of(strip * 256, 256), 256)
        left = jnp.concatenate([row_full[turn, slot, :, window] for slot in slots], axis=0)
        right_side = jnp.concatenate([ordered[slot] for slot in slots], axis=0)
        return window, lax.dot_general(
            left, right_side, (((0,), (0,)), ((), ())), preferred_element_type=jnp.float32
        )

    def first_product(first, last):
        @pl.loop(first, last)
        def _(strip):
            window, values = product(0, range(16), strip)
            gram[window, :] = values

    def gather_product(slots):
        @pl.loop(0, 4)
        def _(strip):
            window, values = product(1, slots, strip)
            gram[window, :] += values

    def last_product(slots):
        @pl.loop(0, 4)
        def _(strip):
            window, values = product(1, slots, strip)
            gram[window, :] = scale * (gram[window, :] + values)

    total[...] = jnp.zeros_like(total)

    @pl.loop(0, FOLD // WIDE_PART)
    def _(step):
        at = step * WIDE_PART
        add_part(val, at, cond, at, at, 0, WIDE_PART)

    merged(total.at[0], merge, cube)
    total[0] = jnp.zeros_like(total[0])
    fill_table(cube, pair_weight(here), table)
    deal(0)
    row_early, col_early = row_spread(0), col_spread(0)
    row_late, col_late = row_spread(1), col_spread(1)
    cube_copy = remote(cube_sent, cube_got, cube_sem.at[0], cube_sem.at[1], next_device)

    def cond_part(chunk):
        add_part(val, HALF + chunk * PART, got_cond, chunk * PART, HALF + chunk * PART, 0)

    def val_part(chunk):
        val_shift(chunk).wait_recv()
        add_part(got_val, chunk * PART, cond, chunk * PART, chunk * PART, 1)

    cond_shift(0).wait_recv()
    cond_part(0)
    val_part(0)
    cond_shift(1).wait_recv()
    cond_part(1)
    val_part(1)
    next(col_early)
    next(row_early)
    cond_shift(2).wait_recv()
    next(row_early)
    cond_part(2)
    merged(total.at[0], merge, cube_sent)
    cube_copy.start()
    next(row_early)
    next(col_early)
    val_part(2)
    merged(total.at[1], merge, cube)
    cube_copy.wait_recv()
    cube[...] += cube_got[...]
    fill_table(cube, pair_weight(before), table)
    next(row_early)
    deal(1)
    next(row_early)
    next(col_early)
    next(row_late)
    next(row_late)
    next(col_late)
    next(col_late)
    next(col_early)
    next(row_early)
    next(row_late)
    next(col_late)
    next(row_late)
    next(col_early)
    next(col_early)
    next(row_late)
    next(row_late)
    next(col_late)
    next(row_early)
    first_product(0, 4)
    next(col_late)
    next(col_late)
    gather_product(
        [col, line(1, 0)]
        + [line(which, offset) for which in range(2) for offset in (1, -1, 2, -2)]
    )
    next(row_late)
    last_product(
        [line(0, 3), line(0, -3), line(0, -4), line(1, 3), line(1, -3), line(1, 4)]
    )
    for turn in range(2):
        for which in range(2):
            dealt(turn, which).wait_send()
    for chunk in range(CHUNKS):
        val_shift(chunk).wait_send()
        cond_shift(chunk).wait_send()
    cube_copy.wait_send()
    for copy in sent:
        copy.wait_send()

def response(valence, conduction, val_energy, cond_energy, sphere_index, scale):
    anywhere = pl.BlockSpec(memory_space=pl.ANY)
    scalars = pl.BlockSpec(memory_space=pltpu.SMEM)
    dma = pltpu.SemaphoreType.DMA
    f32, bf16 = jnp.float32, jnp.bfloat16
    view = (4, FOLD, GRID, GRID)
    return pl.pallas_call(
        functools.partial(panel_kernel, scale),
        out_shape=pltpu.VMEM((1024, 1024), jnp.float32),
        in_specs=[
            anywhere, anywhere, scalars, scalars, pl.BlockSpec(memory_space=pltpu.VMEM), scalars,
            anywhere, anywhere, anywhere, anywhere,
        ],
        out_specs=pl.BlockSpec(memory_space=pltpu.VMEM),
        scratch_shapes=[
            pltpu.VMEM((2, 4, FOLD, GRID, GRID), bf16),
            pltpu.VMEM((FOLD, 3, GRID, 128), bf16),
            pltpu.VMEM((FOLD, 3, GRID, 128), bf16),
            pltpu.VMEM((HALF, 3, GRID, 128), bf16),
            pltpu.VMEM((HALF, 3, GRID, 128), bf16),
            pltpu.VMEM((768, 256), bf16),
            pltpu.VMEM((128, 192), bf16),
            pltpu.VMEM((4, 64, 1024), bf16),
            pltpu.VMEM((256, 256), bf16),
            pltpu.VMEM((2, 4, 2, 2, 4, 32, 128), f32),
            pltpu.VMEM((64, 512), f32),
            pltpu.VMEM((64, 512), f32),
            pltpu.VMEM((64, 512), f32),
            pltpu.VMEM((128, 128), f32),
            pltpu.VMEM((128, 128), jnp.int32),
            pltpu.VMEM((128, 128), f32),
            pltpu.VMEM((128, 256), bf16),
            pltpu.VMEM((2, 16, 16, 128), bf16),
            pltpu.VMEM((2, 16, 16, 128), bf16),
            pltpu.VMEM((2, 16, 16, 128), bf16),
            pltpu.VMEM((256, 128), f32),
            pltpu.VMEM((2, 16, 32, 1024), bf16),
            pltpu.VMEM((2, 16, 32, 1024), bf16),
            pltpu.VMEM((16, 32, 1024), bf16),
            dma((4 * CHUNKS,)),
            dma((4,)),
            dma((2, CHUNKS)),
            dma((2, CHUNKS)),
            dma((2,)),
            dma((2, 2)),
            dma((2, 2)),
            dma((2, 15)),
            dma((2, 16)),
            dma((2, 15)),
            dma((2, 16)),
        ],
        compiler_params=pltpu.CompilerParams(
            collective_id=0, has_side_effects=True, vmem_limit_bytes=59 * 2**20
        ),
        name="response",
    )(
        valence.reshape(view), conduction.reshape(view), val_energy, cond_energy,
        sphere_index.reshape(128, 128), width_table(), depth_table(), height_table(), merge_table(),
        swap_table(),
    )


def finish_kernel(source, target, sem):
    strips = [pl.ds(strip * 256, 256) for strip in range(4)]
    copies = [
        pltpu.make_async_copy(source.at[strip], target.at[strip], sem.at[number])
        for number, strip in enumerate(strips)
    ]
    for copy in copies:
        copy.start()
    for copy in copies:
        copy.wait()


def finished(values):
    return pl.pallas_call(
        finish_kernel,
        out_shape=jax.ShapeDtypeStruct((1024, 1024), jnp.float32),
        in_specs=[pl.BlockSpec(memory_space=pltpu.VMEM)],
        out_specs=pl.BlockSpec(memory_space=pl.ANY),
        scratch_shapes=[pltpu.SemaphoreType.DMA((4,))],
        compiler_params=pltpu.CompilerParams(vmem_limit_bytes=2**20),
        name="finished",
    )(values)


def local(valence, conduction, val_energy, cond_energy, sphere_index):
    devices = lax.axis_size("row") * lax.axis_size("col")
    scale = -1.0 / math.sqrt(2 * devices)
    return finished(
        response(valence, conduction, val_energy, cond_energy, sphere_index, scale)
    )


def solution(mesh):
    placed = (
        P(("row", "col"), None, None, None),
        P(("row", "col"), None, None, None),
        P(),
        P(("row", "col")),
        P(),
    )
    return jax.shard_map(
        local, mesh=mesh, in_specs=placed, out_specs=P("row", "col"), check_vma=False
    )
```
